32 devices in a mesh: gz: 8 (over z, y), gx: 4 (over x, core).
Axes of the slice: x: 2, y: 2, z: 4, core: 2. Of those that a mesh axis runs over, the one named last changes fastest.
Arguments:
- offsets: float32 [4, 64, 3, 64], P('gx', 'gz'), may hold values from 0 to 1
- strength: float32 [4, 64, 64], P('gx', 'gz'), may hold values from -6 to 6
- cells: int32 [4, 64, 3, 64], P('gx', 'gz'), may hold values from 0 to 252, as said below
- counts: int32 [4, 64], P('gx', 'gz'), may hold values from 0 to 64, as said below
- kx_modes: int32 [64], replicated, may hold values from 0 to 511, as said below
- ky_modes: int32 [64], replicated, may hold values from 0 to 511, as said below
Outputs:
- stream: float32 [256, 64, 128], P('gz', 'gx')
The draws below stay inside these ranges and needn't reach their ends.
Inputs may be any that keep to these rules, and one draw needn't show every extreme that they name: `cells`: component 0 lies in 0 to 31, components 1 and 2 in 0 to 252. `counts`: some slot of some device is full in every draw. `kx_modes`: distinct indices. `ky_modes`: distinct indices.
All inputs are finite; a program needn't handle non-finite values.
Results may differ from the reference program's by a relative error of at most 0.0034.
Values sent between devices are 32-bit elements; how exact they have to be, the bound alone decides.
No kernel may reach another device: no remote copies, remote signals or barrier semaphores. Data moves between devices by JAX's collectives and lax.ppermute only.
A program may use at most 128 MiB of HBM per device.

```python
import jax
import jax.numpy as jnp
from jax import lax

NXD = 512
KX = 64
KY = 64
ZDEV = 32
CAP = 64
N_GZ = 8
N_GX = 4


def draw_cells(key, part):
    key = jax.random.fold_in(key, 11)
    key_z, key_xy = jax.random.split(key)
    along_z = jax.random.randint(key_z, (N_GX, N_GZ * N_GZ, 1, CAP), 0, ZDEV)
    along_xy = jax.random.randint(key_xy, (N_GX, N_GZ * N_GZ, 2, CAP), 0, NXD // 2 - 3)
    return jnp.concatenate([along_z, along_xy], axis=2).astype(jnp.int32)


def draw_counts(key, part):
    key = jax.random.fold_in(key, 12)
    key_load, key_rows, key_full = jax.random.split(key, 3)
    factor = jax.random.randint(key_load, (N_GZ,), 1, 5)
    limit = jnp.tile(CAP * factor // 4, N_GZ)[None, :] * jnp.ones((N_GX, 1), jnp.int32)
    drawn = jax.random.randint(key_rows, (N_GX, N_GZ * N_GZ), limit // 2, limit + 1)
    where_full = jax.random.randint(key_full, (), 0, N_GX * N_GZ * N_GZ)
    return drawn.reshape(-1).at[where_full].set(CAP).reshape(N_GX, N_GZ * N_GZ).astype(jnp.int32)


def draw_kx_modes(key, part):
    key = jax.random.fold_in(key, 13)
    chosen = jax.random.permutation(key, 2 * KX)[:KX] - KX
    return (chosen % NXD).astype(jnp.int32)


def draw_ky_modes(key, part):
    key = jax.random.fold_in(key, 14)
    chosen = jax.random.permutation(key, 2 * KY)[:KY] - KY
    return (chosen % NXD).astype(jnp.int32)


def block_levels(rng, shape, cuts, least, top_value):
    def one(dim, parts):
        heights = jax.random.uniform(jax.random.fold_in(jax.random.fold_in(rng, 6), dim), (parts,), jnp.float32, least / len(cuts), top_value / len(cuts))
        return jnp.repeat(jnp.exp(heights), shape[dim] // parts).reshape((-1,) + (1,) * (len(shape) - dim - 1))

    loudness = one(*cuts[0])
    for cut in cuts[1:]:
        loudness = loudness * one(*cut)
    return loudness


def centred(rng, shape, spread, reach, cuts=(), held_as=jnp.bfloat16):
    loudness = block_levels(rng, shape, cuts, -0.22, 0.18) if cuts else 1.0
    values = jax.random.normal(rng, shape, jnp.float32) * spread * loudness
    return jnp.minimum(jnp.maximum(values, -reach), reach).astype(held_as)


def setup_inputs(seed: int = 0) -> dict:
    splits = jax.random.split(jax.random.key(seed), 7)
    offsets = jnp.clip(1.0 * jax.random.uniform(splits[0], (N_GX, N_GZ * N_GZ, 3, CAP), jnp.float32) ** block_levels(splits[0], (N_GX, N_GZ * N_GZ, 3, CAP), ((0, 4), (1, 8)), -0.2, 0.2), 0.0, 1.0)
    strength = centred(splits[1], (N_GX, N_GZ * N_GZ, CAP), 1.0, 6.0, ((0, 4), (1, 8)), jnp.float32)
    cells = draw_cells(jax.random.fold_in(splits[6], 71), 0)
    counts = draw_counts(jax.random.fold_in(splits[6], 71), 0)
    kx_modes = draw_kx_modes(jax.random.fold_in(splits[6], 71), 0)
    ky_modes = draw_ky_modes(jax.random.fold_in(splits[6], 71), 0)
    return dict(offsets=offsets, strength=strength, cells=cells, counts=counts, kx_modes=kx_modes, ky_modes=ky_modes)


def near_part(dist):
    return 1.0 - 2.5 * dist * dist + 1.5 * dist * dist * dist

def far_part(dist):
    return 0.5 * (2.0 - dist) * (2.0 - dist) * (1.0 - dist)

def kernel_weights(frac):
    return jnp.stack([far_part(1.0 + frac), near_part(frac), near_part(1.0 - frac), far_part(2.0 - frac)])

def spectra(planes, kx_list, ky_list, length):
    cells_along = planes.shape[1]
    position = jnp.arange(cells_along, dtype=jnp.int32)
    phase_x = (kx_list[:, None] * position[None, :] % length).astype(jnp.float32) * (2.0 * jnp.pi / length)
    phase_y = (ky_list[:, None] * position[None, :] % length).astype(jnp.float32) * (2.0 * jnp.pi / length)
    cos_x, sin_x = (jnp.cos(phase_x), jnp.sin(phase_x))
    cos_y, sin_y = (jnp.cos(phase_y), jnp.sin(phase_y))
    high = lax.Precision.HIGHEST
    real_b = jnp.einsum('kx,zxy->zky', cos_x, planes, precision=high)
    imag_b = -jnp.einsum('kx,zxy->zky', sin_x, planes, precision=high)
    real_f = jnp.einsum('zky,qy->zkq', real_b, cos_y, precision=high) + jnp.einsum('zky,qy->zkq', imag_b, sin_y, precision=high)
    imag_f = jnp.einsum('zky,qy->zkq', imag_b, cos_y, precision=high) - jnp.einsum('zky,qy->zkq', real_b, sin_y, precision=high)
    return jnp.concatenate([real_f, imag_f], axis=2) * (1.0 / cells_along)

def green_terms(kx_list, ky_list, length, sigma):
    half = length // 2
    signed_x = jnp.where(kx_list >= half, kx_list - length, kx_list).astype(jnp.float32)
    signed_y = jnp.where(ky_list >= half, ky_list - length, ky_list).astype(jnp.float32)
    step = 2.0 * jnp.pi / length
    kappa = jnp.sqrt(sigma * sigma + step * step * (signed_x[:, None] ** 2 + signed_y[None, :] ** 2))
    return (kappa, sigma / kappa)

def reference(offsets, strength, cells, counts, kx_modes, ky_modes):
    planes_all = ZDEV * N_GZ
    cells_along = NXD // 2
    off_five = offsets.reshape(N_GX, N_GZ, N_GZ, 3, CAP)
    str_four = strength.reshape(N_GX, N_GZ, N_GZ, CAP)
    cell_five = cells.reshape(N_GX, N_GZ, N_GZ, 3, CAP)
    count_three = counts.reshape(N_GX, N_GZ, N_GZ)
    nodes = jnp.arange(4, dtype=jnp.int32)

    def deposit(total, slab):
        frac = lax.dynamic_index_in_dim(off_five, slab, 2, keepdims=False)
        power = lax.dynamic_index_in_dim(str_four, slab, 2, keepdims=False)
        base = lax.dynamic_index_in_dim(cell_five, slab, 2, keepdims=False)
        number = lax.dynamic_index_in_dim(count_three, slab, 2, keepdims=False)
        live = jnp.arange(CAP, dtype=jnp.int32)[None, None, :] < number[..., None]
        weight_s = jnp.where(live, power, 0.0).reshape(-1)
        frac_rows = jnp.transpose(frac, (2, 0, 1, 3)).reshape(3, -1)
        base_rows = jnp.transpose(base, (2, 0, 1, 3)).reshape(3, -1)
        weight_z = kernel_weights(frac_rows[0])
        weight_x = kernel_weights(frac_rows[1])
        weight_y = kernel_weights(frac_rows[2])
        left = ((weight_s[None, :] * weight_z)[:, None, :] * weight_x[None, :, :]).astype(jnp.bfloat16).astype(jnp.float32)
        right = weight_y.astype(jnp.bfloat16).astype(jnp.float32)
        values = left[:, :, None, :] * right[None, None, :, :]
        z_index = (base_rows[0][None, :] + nodes[:, None] + slab * ZDEV).astype(jnp.int32)
        x_index = (base_rows[1][None, :] + nodes[:, None]).astype(jnp.int32)
        y_index = (base_rows[2][None, :] + nodes[:, None]).astype(jnp.int32)
        shape = values.shape
        total = total.at[jnp.broadcast_to(z_index[:, None, None, :], shape), jnp.broadcast_to(x_index[None, :, None, :], shape), jnp.broadcast_to(y_index[None, None, :, :], shape)].add(values)
        return (total, None)
    start_grid = jnp.zeros((planes_all + 3, cells_along, cells_along), jnp.float32)
    full_grid, _ = lax.scan(deposit, start_grid, jnp.arange(N_GZ, dtype=jnp.int32))
    spectrum = spectra(full_grid[:planes_all], kx_modes, ky_modes, NXD)
    sigma = 4.0 / planes_all
    kappa, amplitude = green_terms(kx_modes, ky_modes, NXD, sigma)
    spec_four = spectrum.reshape(planes_all, KX, 2, KY)
    sources = jnp.arange(planes_all, dtype=jnp.int32)

    def one_plane(target):
        distance = jnp.abs(target - sources).astype(jnp.float32)
        green = amplitude[None] * jnp.exp(-kappa[None] * distance[:, None, None])
        return jnp.einsum('bky,bkcy->kcy', green, spec_four, precision=lax.Precision.HIGHEST).reshape(KX, 2 * KY)
    return lax.map(one_plane, sources)
```

```python
import functools
import math

import jax
import jax.numpy as jnp
from jax import lax
from jax.experimental import pallas as pl
from jax.experimental.pallas import tpu as pltpu
from jax.sharding import PartitionSpec as P

NXD = 512
ZDEV = 32
SPILL = 3
PLANES = ZDEV + SPILL

SIN_HALF = (3.14158202, -5.16714279, 2.54189899, -0.55463611)
COS_HALF = (0.99999995, -4.93479286, 4.05841191, -1.33188015, 0.21969677)


def poly(u, coefs):
    total = jnp.full_like(u, coefs[-1])
    for c in coefs[-2::-1]:
        total = total * u + c
    return total


def cos_sin_turns(turns):
    r = turns - jnp.round(turns)
    u = r * r
    s = r * poly(u, SIN_HALF)
    c2 = poly(u, tuple(2.0 * c for c in COS_HALF))
    return 1.0 - 2.0 * s * s, s * c2


def node_weights(f):
    g = 1.0 - f
    fg = -0.5 * f * g
    return (
        fg * g,
        1.0 + f * f * (1.5 * f - 2.5),
        1.0 + g * g * (1.5 * g - 2.5),
        fg * f,
    )


def node_phasors(freq):
    c1, s1 = cos_sin_turns(freq)
    c2, s2 = c1 * c1 - s1 * s1, 2.0 * c1 * s1
    return ((c1, s1), (c2, s2), (c1 * c2 - s1 * s2, s1 * c2 + c1 * s2))


def transform(freq, nodes, base, weights):
    c, s = cos_sin_turns(freq * base)
    (c1, s1), (c2, s2), (c3, s3) = nodes
    w0, w1, w2, w3 = weights
    re = w0 + w1 * c1 + w2 * c2 + w3 * c3
    im = w1 * s1 + w2 * s2 + w3 * s3
    return c * re - s * im, s * re + c * im


def spectrum_kernel(group, slab_ref, rows_ref, kx_ref, ky_ref, kappa_ref, near_ref, send_ref, acc_ref):
    kx_count = kx_ref.shape[0]
    ky_count = ky_ref.shape[0]
    blocks = rows_ref.shape[0] // 8
    kx, ky = kx_ref[...], ky_ref[...]
    kx_nodes, ky_nodes = node_phasors(kx), node_phasors(ky)
    low_lanes = lax.broadcasted_iota(jnp.int32, (4, 128), 1) < 64
    plane = lax.broadcasted_iota(jnp.int32, (40, 128), 0).astype(jnp.float32)

    def one_block(block):
        rows = rows_ref[pl.ds(pl.multiple_of(block * 8, 8), 8), :]
        turned = pltpu.roll(rows, 64, axis=1)
        left = jnp.where(low_lanes, rows[0:4], turned[4:8])
        right = jnp.where(low_lanes, turned[0:4], rows[4:8])
        w_left = node_weights(left)
        w_right = node_weights(right)
        strength = right[1:2]
        base_z, base_y = left[2:3], left[3:4]
        base_x = right[2:3]
        wz = [w[0:1] * strength for w in w_left]
        wy = [w[1:2].astype(jnp.bfloat16).astype(jnp.float32) for w in w_left]
        wx = [w[0:1] for w in w_right]
        dist = plane - base_z
        spread = jnp.where(
            dist == 0.0,
            wz[0],
            jnp.where(dist == 1.0, wz[1], jnp.where(dist == 2.0, wz[2], jnp.where(dist == 3.0, wz[3], 0.0))),
        )
        cx, sx = transform(kx, kx_nodes, base_x, wx)
        cy, sy = transform(ky, ky_nodes, base_y, wy)
        x_both = jnp.concatenate([cx, sx], axis=1)
        spread_both = jnp.concatenate([spread, spread], axis=1)
        lhs = jnp.concatenate(
            [(spread_both[z : z + 1] * x_both).astype(jnp.bfloat16) for z in range(PLANES)], axis=0
        )
        exact = jnp.concatenate(
            [jnp.concatenate([cy, -sy], axis=1), jnp.concatenate([-sy, -cy], axis=1)], axis=0
        )
        high = exact.astype(jnp.bfloat16)
        low = (exact - high.astype(jnp.float32)).astype(jnp.bfloat16)
        return lhs, jnp.concatenate([high, low], axis=0)

    def step(index, _):
        pieces = [one_block(index * group + j) for j in range(group)]
        lhs = jnp.concatenate([p[0] for p in pieces], axis=1)
        rhs = jnp.concatenate([p[1] for p in pieces], axis=1)
        product = lax.dot_general(lhs, rhs, (((1,), (1,)), ((), ())), preferred_element_type=jnp.float32)

        @pl.when(index == 0)
        def _():
            acc_ref[...] = product

        @pl.when(index > 0)
        def _():
            acc_ref[...] += product

        return 0

    lax.fori_loop(0, blocks // group, step, 0)

    slab = slab_ref[0]
    slabs = send_ref.shape[0]
    decay = jnp.exp(-kappa_ref[...])
    width = 2 * ky_count

    def plane_of(z):
        both = acc_ref[z * kx_count : (z + 1) * kx_count, :]
        return both[:, :width] + both[:, width:]

    inside = jnp.where(slab < slabs - 1, 1.0, 0.0)
    spilled = [plane_of(ZDEV + j) * inside for j in range(SPILL)]
    down = spilled[2]
    down = spilled[1] + decay * down
    down = spilled[0] + decay * down
    for z in range(ZDEV - 1, -1, -1):
        down = decay * down
        near_ref[z] = down
        down = plane_of(z) + down
    up = jnp.zeros_like(decay)
    for z in range(ZDEV):
        up = plane_of(z) + decay * up
        near_ref[z] += up
    up_near = spilled[0] + decay * up
    up_far = spilled[2] + decay * (spilled[1] + decay * up_near)
    for target in range(slabs):
        send_ref[target, 0] = jnp.where(
            target < slab, down, jnp.where(target == slab + 1, up_near, up_far)
        )
        send_ref[target, 1] = spilled[1]
        send_ref[target, 2] = spilled[2]


def far_kernel(slab_ref, near_ref, received_ref, kappa_ref, out_ref, powers_ref):
    slab = slab_ref[0]
    slabs = received_ref.shape[0]
    kappa = kappa_ref[...]
    decay = jnp.exp(-kappa)
    sigma = 4.0 / (ZDEV * slabs)
    scale = (sigma * 2.0 / NXD) / kappa
    low = jnp.zeros_like(kappa)
    high = jnp.zeros_like(kappa)
    first = jnp.zeros_like(kappa)
    second = jnp.zeros_like(kappa)
    for source in range(slabs):
        gap = slab - source
        reach = jnp.where(
            gap > 1,
            ZDEV * gap - (PLANES - 1),
            jnp.where(gap < 0, ZDEV * (-gap - 1), 0),
        ).astype(jnp.float32)
        moment = jnp.exp(-kappa * reach) * received_ref[source, 0]
        low = low + jnp.where(gap > 0, moment, 0.0)
        high = high + jnp.where(gap < 0, moment, 0.0)
        first = first + jnp.where(gap == 1, received_ref[source, 1], 0.0)
        second = second + jnp.where(gap == 1, received_ref[source, 2], 0.0)
    high = high * scale
    low = low * scale
    first = first * scale
    second = second * scale
    for z in range(ZDEV - 1, -1, -1):
        high = decay * high
        powers_ref[z] = high
    extra = {0: decay * (first + decay * second), 1: decay * second}
    source_at = {1: first, 2: second}
    for z in range(ZDEV):
        if z:
            low = decay * low
        if z in source_at:
            low = low + source_at[z]
        total = scale * near_ref[z] + low + powers_ref[z]
        if z in extra:
            total = total + extra[z]
        out_ref[z] = total


def shards(offsets, strength, cells, counts, kx_modes, ky_modes):
    slabs = lax.axis_size("gz")
    x_groups = lax.axis_size("gx")
    cap = strength.shape[-1]
    slab = lax.axis_index("gz").astype(jnp.int32).reshape(1)

    live = jnp.arange(cap, dtype=jnp.int32)[None, :] < counts[0][:, None]
    power = jnp.where(live, strength[0], 0.0)
    place = cells[0].astype(jnp.float32)
    frac = offsets[0]
    rows = jnp.stack(
        [
            jnp.concatenate([frac[:, 0], frac[:, 1]], axis=1),
            jnp.concatenate([frac[:, 2], power], axis=1),
            jnp.concatenate([place[:, 0], place[:, 1]], axis=1),
            jnp.concatenate([place[:, 2], jnp.zeros_like(power)], axis=1),
        ],
        axis=1,
    )
    sent = jnp.broadcast_to(rows[:, None], (slabs, x_groups, 4, 128)).reshape(slabs * x_groups, 4, 128)
    arrived = lax.all_to_all(sent, ("gz", "gx"), split_axis=0, concat_axis=0, tiled=True)
    arrived = arrived.reshape(-1, 128)

    kx_local = kx_modes.shape[0] // x_groups
    ky_count = ky_modes.shape[0]
    own_kx = lax.dynamic_slice_in_dim(kx_modes, lax.axis_index("gx") * kx_local, kx_local)
    kx_turns = jnp.broadcast_to((own_kx.astype(jnp.float32) / NXD)[:, None], (kx_local, 128))
    ky_turns = jnp.broadcast_to((ky_modes.astype(jnp.float32) / NXD)[:, None], (ky_count, 128))
    signed_x = jnp.where(own_kx >= NXD // 2, own_kx - NXD, own_kx).astype(jnp.float32)
    signed_y = jnp.where(ky_modes >= NXD // 2, ky_modes - NXD, ky_modes).astype(jnp.float32)
    signed_y = jnp.concatenate([signed_y, signed_y])
    sigma = 4.0 / (ZDEV * slabs)
    step = 2.0 * math.pi / NXD
    kappa = jnp.sqrt(sigma * sigma + step * step * (signed_x[:, None] ** 2 + signed_y[None, :] ** 2))

    width = 2 * ky_count
    blocks = arrived.shape[0] // 8
    group = math.gcd(blocks, 2)
    smem = pl.BlockSpec(memory_space=pltpu.SMEM)
    vmem = pl.BlockSpec(memory_space=pltpu.VMEM)
    near, moments = pl.pallas_call(
        functools.partial(spectrum_kernel, group),
        out_shape=(
            jax.ShapeDtypeStruct((ZDEV, kx_local, width), jnp.float32),
            jax.ShapeDtypeStruct((slabs, SPILL, kx_local, width), jnp.float32),
        ),
        in_specs=[smem, vmem, vmem, vmem, vmem],
        out_specs=(vmem, vmem),
        scratch_shapes=[pltpu.VMEM((PLANES * kx_local, 2 * width), jnp.float32)],
        compiler_params=pltpu.CompilerParams(vmem_limit_bytes=32 * 1024 * 1024),
    )(slab, arrived, kx_turns, ky_turns, kappa)

    received = lax.all_to_all(moments, "gz", split_axis=0, concat_axis=0, tiled=True)
    return pl.pallas_call(
        far_kernel,
        out_shape=jax.ShapeDtypeStruct((ZDEV, kx_local, width), jnp.float32),
        in_specs=[smem, vmem, vmem, vmem],
        out_specs=vmem,
        scratch_shapes=[pltpu.VMEM((ZDEV, kx_local, width), jnp.float32)],
        compiler_params=pltpu.CompilerParams(vmem_limit_bytes=32 * 1024 * 1024),
    )(slab, near, received, kappa)


def solution(mesh):
    placed = (
        P("gx", "gz", None, None),
        P("gx", "gz", None),
        P("gx", "gz", None, None),
        P("gx", "gz"),
        P(),
        P(),
    )
    return jax.shard_map(
        shards, mesh=mesh, in_specs=placed, out_specs=P("gz", "gx", None), check_vma=False
    )
```

```python
import functools
import math

import jax
import jax.numpy as jnp
from jax import lax
from jax.experimental import pallas as pl
from jax.experimental.pallas import tpu as pltpu
from jax.sharding import PartitionSpec as P

NXD = 512
ZDEV = 32
SPILL = 3
PLANES = ZDEV + SPILL

SIN_HALF = tuple(math.sqrt(2.0) * c for c in (3.14158202, -5.16714279, 2.54189899, -0.55463611))
COS_HALF = tuple(math.sqrt(2.0) * c for c in (0.9999933, -4.93393801, 4.04128375, -1.22212681))


def poly(u, coefs):
    total = jnp.full_like(u, coefs[-1])
    for c in coefs[-2::-1]:
        total = total * u + c
    return total


def cos_sin_turns(turns):
    r = turns - jnp.round(turns)
    u = r * r
    s = r * poly(u, SIN_HALF)
    return 1.0 - s * s, s * poly(u, COS_HALF)


def node_weights(f):
    g = 1.0 - f
    fg = -0.5 * f * g
    return (
        fg * g,
        1.0 + f * f * (1.5 * f - 2.5),
        1.0 + g * g * (1.5 * g - 2.5),
        fg * f,
    )


def node_phasors(freq):
    return cos_sin_turns(0.5 * freq) + cos_sin_turns(1.5 * freq)


def transform(freq, nodes, middle, pairs):
    c, s = cos_sin_turns(freq * middle)
    c1, s1, c3, s3 = nodes
    even1, odd1, even3, odd3 = pairs
    re = even1 * c1 + even3 * c3
    im = odd1 * s1 + odd3 * s3
    return c * re - s * im, s * re + c * im


def node_pairs(weights):
    w0, w1, w2, w3 = weights
    return w1 + w2, w2 - w1, w0 + w3, w3 - w0


def two_parts(x):
    high = x.astype(jnp.bfloat16)
    return high, (x - high.astype(jnp.float32)).astype(jnp.bfloat16)


def pack_kernel(counts_ref, offsets_ref, strength_ref, cells_ref, sent_ref):
    slabs, cap = strength_ref.shape
    rows = sent_ref.shape[0] // slabs
    slot = lax.broadcasted_iota(jnp.int32, (slabs, cap), 0)
    lane = lax.broadcasted_iota(jnp.int32, (slabs, cap), 1)
    count = jnp.zeros((slabs, cap), jnp.int32)
    for d in range(slabs):
        count = jnp.where(slot == d, counts_ref[0, d], count)
    power = jnp.where(lane < count, strength_ref[...], 0.0)
    for part in range(4):
        if part < 3:
            low, high = offsets_ref[part], cells_ref[part].astype(jnp.float32)
        else:
            low, high = power, jnp.zeros_like(power)
        own = jnp.concatenate([low, high], axis=1)
        far = jnp.concatenate([own[slabs // 2 :], own[: slabs // 2]], axis=0)
        for copy in range(rows // 8):
            sent_ref[pl.ds(copy * 8 + part, slabs, stride=rows), :] = own
            sent_ref[pl.ds(copy * 8 + 4 + part, slabs, stride=rows), :] = far


def partner(index, step, count):
    return index ^ step if count & (count - 1) == 0 else (index + step) % count


def spectrum_kernel(group, slabs, slab_ref, rows_ref, kx_ref, ky_ref, kappa_ref, near_ref, *rest):
    send_refs, (own_ref, far_ref) = rest[:-2], rest[-2:]
    kx_count = kx_ref.shape[0]
    ky_count = ky_ref.shape[0]
    blocks = rows_ref.shape[0] // 16
    kx, ky = kx_ref[...], ky_ref[...]
    kx_nodes, ky_nodes = node_phasors(kx), node_phasors(ky)
    low_lanes = lax.broadcasted_iota(jnp.int32, (8, 128), 1) < 64
    plane = lax.broadcasted_iota(jnp.int32, (40, 128), 0).astype(jnp.float32)

    def operands(frac, cell, weights, row):
        strength = frac[row + 3 : row + 4]
        base_z = cell[row : row + 1]
        middle_x, middle_y = cell[row + 1 : row + 2] + 1.5, cell[row + 2 : row + 3] + 1.5
        wz = [w[row : row + 1] * strength for w in weights]
        wx = node_pairs([w[row + 1 : row + 2] for w in weights])
        wy = node_pairs([w[row + 2 : row + 3].astype(jnp.bfloat16).astype(jnp.float32) for w in weights])
        dist = plane - base_z
        spread = jnp.where(
            dist == 0.0,
            wz[0],
            jnp.where(dist == 1.0, wz[1], jnp.where(dist == 2.0, wz[2], jnp.where(dist == 3.0, wz[3], 0.0))),
        )
        cx, sx = transform(kx, kx_nodes, middle_x, wx)
        cy, sy = transform(ky, ky_nodes, middle_y, wy)
        lhs = []
        for z in range(PLANES):
            here = jnp.broadcast_to(spread[z : z + 1], cx.shape)
            lhs.append(
                jnp.concatenate([(here * cx).astype(jnp.bfloat16), (here * sx).astype(jnp.bfloat16)], axis=1)
            )
        cy_high, cy_low = two_parts(cy)
        sy_high, sy_low = two_parts(-sy)
        rhs = [
            jnp.concatenate(pair, axis=1)
            for pair in ((cy_high, sy_high), (sy_high, -cy_high), (cy_low, sy_low), (sy_low, -cy_low))
        ]
        return jnp.concatenate(lhs, axis=0), jnp.concatenate(rhs, axis=0)

    def one_block(block):
        rows = rows_ref[pl.ds(pl.multiple_of(block * 16, 16), 16), :]
        turned = pltpu.roll(rows, 64, axis=1)
        frac = jnp.where(low_lanes, rows[0:8], turned[8:16])
        cell = jnp.where(low_lanes, turned[0:8], rows[8:16])
        weights = node_weights(frac)
        return operands(frac, cell, weights, 0), operands(frac, cell, weights, 4)

    def step(index, _):
        pieces = [one_block(index * group + j) for j in range(group)]
        for part, acc_ref in enumerate((own_ref, far_ref)):
            lhs = jnp.concatenate([p[part][0] for p in pieces], axis=1)
            rhs = jnp.concatenate([p[part][1] for p in pieces], axis=1)
            product = lax.dot_general(
                lhs, rhs, (((1,), (1,)), ((), ())), preferred_element_type=jnp.float32
            )

            @pl.when(index == 0)
            def _():
                acc_ref[...] = product

            @pl.when(index > 0)
            def _():
                acc_ref[...] += product

        return 0

    lax.fori_loop(0, blocks // group, step, 0)

    half = slabs // 2
    slab = slab_ref[0]
    upper = slab >= half
    first = jnp.where(upper, half, 0)
    member = slab - first
    far_slab = jnp.where(upper, slab - half, slab + half)
    kappa = kappa_ref[...]
    decay = jnp.exp(-kappa)
    width = 2 * ky_count

    def plane_of(acc_ref, z):
        start = z * kx_count
        both = acc_ref[pl.ds(start if isinstance(z, int) else pl.multiple_of(start, kx_count), kx_count), :]
        return both[:, :width] + both[:, width:]

    def spills_of(acc_ref, index):
        inside = jnp.where(index < slabs - 1, 1.0, 0.0)
        return [plane_of(acc_ref, ZDEV + j) * inside for j in range(SPILL)]

    spilled = spills_of(own_ref, slab)
    down = spilled[0] + decay * (spilled[1] + decay * spilled[2])
    for z in range(ZDEV - 1, -1, -1):
        down = decay * down
        near_ref[z] = down
        down = plane_of(own_ref, z) + down
    up = jnp.zeros_like(decay)
    for z in range(ZDEV):
        up = plane_of(own_ref, z) + decay * up
        near_ref[z] += up
    up_near = spilled[0] + decay * up
    up_far = spilled[2] + decay * (spilled[1] + decay * up_near)

    far_spilled = spills_of(far_ref, far_slab)
    moment = jnp.where(
        upper, jnp.zeros_like(decay), far_spilled[0] + decay * (far_spilled[1] + decay * far_spilled[2])
    )
    for j in range(ZDEV):
        moment = plane_of(far_ref, jnp.where(upper, j, ZDEV - 1 - j)) + decay * moment
    far_near = far_spilled[0] + decay * moment
    far_far = far_spilled[2] + decay * (far_spilled[1] + decay * far_near)

    for hop, send_ref in enumerate(send_refs):
        target = first + partner(member, hop, half)
        zero = jnp.zeros_like(decay)
        ahead = target - slab
        reach = jnp.where(
            ahead > 1, ZDEV * ahead - (PLANES - 1), jnp.where(ahead < 0, ZDEV * (-ahead - 1), 0)
        )
        own_weight = jnp.exp(-kappa * reach.astype(jnp.float32))
        own_low = jnp.where(ahead > 0, own_weight * jnp.where(ahead == 1, up_near, up_far), zero)
        own_high = jnp.where(ahead < 0, own_weight * down, zero)
        far_ahead = target - far_slab
        far_reach = jnp.where(
            far_ahead > 1, ZDEV * far_ahead - (PLANES - 1), jnp.where(far_ahead < 0, ZDEV * (-far_ahead - 1), 0)
        )
        far_weight = jnp.exp(-kappa * far_reach.astype(jnp.float32))
        far_low = jnp.where(upper, far_weight * jnp.where(far_ahead == 1, far_near, far_far), zero)
        far_high = jnp.where(upper, zero, far_weight * moment)
        send_ref[0] = own_low + far_low
        send_ref[1] = own_high + far_high
        for j in (1, 2):
            send_ref[1 + j] = jnp.where(
                ahead == 1, spilled[j], jnp.where(far_ahead == 1, far_spilled[j], zero)
            )


def far_kernel(slabs, kappa_ref, near_ref, *rest):
    received_refs, out_ref, powers_ref = rest[:-2], rest[-2], rest[-1]
    kappa = kappa_ref[...]
    decay = jnp.exp(-kappa)
    sigma = 4.0 / (ZDEV * slabs)
    scale = (sigma * 2.0 / NXD) / kappa
    low, high, first, second = (sum(ref[part] for ref in received_refs) * scale for part in range(4))
    for z in range(ZDEV - 1, -1, -1):
        high = decay * high
        powers_ref[z] = high
    extra = {0: decay * (first + decay * second), 1: decay * second}
    source_at = {1: first, 2: second}
    for z in range(ZDEV):
        if z:
            low = decay * low
        if z in source_at:
            low = low + source_at[z]
        total = scale * near_ref[z] + low + powers_ref[z]
        if z in extra:
            total = total + extra[z]
        out_ref[z] = total


def shards(offsets, strength, cells, counts, kx_modes, ky_modes):
    slabs = lax.axis_size("gz")
    x_groups = lax.axis_size("gx")
    half = slabs // 2
    cap = strength.shape[-1]
    slab = lax.axis_index("gz").astype(jnp.int32).reshape(1)

    smem = pl.BlockSpec(memory_space=pltpu.SMEM)
    vmem = pl.BlockSpec(memory_space=pltpu.VMEM)
    sent = pl.pallas_call(
        pack_kernel,
        out_shape=jax.ShapeDtypeStruct((slabs * x_groups * 8, 2 * cap), jnp.float32),
        in_specs=[smem, vmem, vmem, vmem],
        out_specs=vmem,
    )(counts, jnp.transpose(offsets[0], (1, 0, 2)), strength[0], jnp.transpose(cells[0], (1, 0, 2)))
    sent = sent.reshape(slabs * x_groups, 8, 2 * cap)
    arrived = lax.all_to_all(sent, ("gz", "gx"), split_axis=0, concat_axis=0, tiled=True)
    arrived = arrived.reshape(-1, 128)

    kx_local = kx_modes.shape[0] // x_groups
    ky_count = ky_modes.shape[0]
    own_kx = lax.dynamic_slice_in_dim(kx_modes, lax.axis_index("gx") * kx_local, kx_local)
    kx_turns = jnp.broadcast_to((own_kx.astype(jnp.float32) / NXD)[:, None], (kx_local, 128))
    ky_turns = jnp.broadcast_to((ky_modes.astype(jnp.float32) / NXD)[:, None], (ky_count, 128))
    signed_x = jnp.where(own_kx >= NXD // 2, own_kx - NXD, own_kx).astype(jnp.float32)
    signed_y = jnp.where(ky_modes >= NXD // 2, ky_modes - NXD, ky_modes).astype(jnp.float32)
    signed_y = jnp.concatenate([signed_y, signed_y])
    sigma = 4.0 / (ZDEV * slabs)
    step = 2.0 * math.pi / NXD
    kappa = jnp.sqrt(sigma * sigma + step * step * (signed_x[:, None] ** 2 + signed_y[None, :] ** 2))

    width = 2 * ky_count
    blocks = arrived.shape[0] // 16
    group = math.gcd(blocks, 16)
    planes = jax.ShapeDtypeStruct((ZDEV, kx_local, width), jnp.float32)
    message = jax.ShapeDtypeStruct((4, kx_local, width), jnp.float32)
    acc = pltpu.VMEM((PLANES * kx_local, 2 * width), jnp.float32)
    near, *messages = pl.pallas_call(
        functools.partial(spectrum_kernel, group, slabs),
        out_shape=(planes,) + (message,) * half,
        in_specs=[smem, vmem, vmem, vmem, vmem],
        out_specs=(vmem,) * (1 + half),
        scratch_shapes=[acc, acc],
        compiler_params=pltpu.CompilerParams(vmem_limit_bytes=40 * 1024 * 1024),
    )(slab, arrived, kx_turns, ky_turns, kappa)

    received = messages[:1]
    for hop in range(1, half):
        pairs = [(i, i - i % half + partner(i % half, hop, half)) for i in range(slabs)]
        received.append(lax.ppermute(messages[hop], "gz", pairs))
    return pl.pallas_call(
        functools.partial(far_kernel, slabs),
        out_shape=planes,
        in_specs=[vmem] * (2 + half),
        out_specs=vmem,
        scratch_shapes=[pltpu.VMEM((ZDEV, kx_local, width), jnp.float32)],
        compiler_params=pltpu.CompilerParams(vmem_limit_bytes=32 * 1024 * 1024),
    )(kappa, near, *received)


def solution(mesh):
    placed = (
        P("gx", "gz", None, None),
        P("gx", "gz", None),
        P("gx", "gz", None, None),
        P("gx", "gz"),
        P(),
        P(),
    )
    return jax.shard_map(
        shards, mesh=mesh, in_specs=placed, out_specs=P("gz", "gx", None), check_vma=False
    )
```

```python
import functools
import math

import jax
import jax.numpy as jnp
from jax import lax
from jax.experimental import pallas as pl
from jax.experimental.pallas import tpu as pltpu
from jax.sharding import PartitionSpec as P

NXD = 512
ZDEV = 32
SPILL = 3
PLANES = ZDEV + SPILL
MIDDLE = 126.0
FINE = 2

SIN_HALF = tuple(math.sqrt(2.0) * c for c in (3.14158202, -5.16714279, 2.54189899, -0.55463611))
COS_HALF = tuple(math.sqrt(2.0) * c for c in (0.9999933, -4.93393801, 4.04128375, -1.22212681))


def poly(u, coefs):
    total = jnp.full_like(u, coefs[-1])
    for c in coefs[-2::-1]:
        total = total * u + c
    return total


def cos_sin_turns(turns):
    r = turns - jnp.round(turns)
    u = r * r
    s = r * poly(u, SIN_HALF)
    return 1.0 - s * s, s * poly(u, COS_HALF)


def node_weights(f):
    g = 1.0 - f
    fg = -0.5 * f * g
    return (
        fg * g,
        1.0 + f * f * (1.5 * f - 2.5),
        1.0 + g * g * (1.5 * g - 2.5),
        fg * f,
    )


def node_phasors(freq):
    return cos_sin_turns(0.5 * freq) + cos_sin_turns(1.5 * freq)


def transform(table_ref, nodes, column, side, pairs):
    column = jnp.broadcast_to(column, table_ref.shape[1:])
    c = jnp.take_along_axis(table_ref[0], column, axis=1)
    s = jnp.take_along_axis(table_ref[1], column, axis=1) * side
    c1, s1, c3, s3 = nodes
    even1, odd1, even3, odd3 = pairs
    re = even1 * c1 + even3 * c3
    im = odd1 * s1 + odd3 * s3
    return c * re - s * im, s * re + c * im


def node_pairs(weights):
    w0, w1, w2, w3 = weights
    return w1 + w2, w2 - w1, w0 + w3, w3 - w0


def two_parts(x):
    high = x.astype(jnp.bfloat16)
    return high, (x - high.astype(jnp.float32)).astype(jnp.bfloat16)


def pack_kernel(counts_ref, offsets_ref, strength_ref, cells_ref, sent_ref):
    slabs, cap = strength_ref.shape
    rows = sent_ref.shape[0] // slabs
    slot = lax.broadcasted_iota(jnp.int32, (slabs, cap), 0)
    lane = lax.broadcasted_iota(jnp.int32, (slabs, cap), 1)
    count = jnp.zeros((slabs, cap), jnp.int32)
    for d in range(slabs):
        count = jnp.where(slot == d, counts_ref[0, d], count)
    power = jnp.where(lane < count, strength_ref[...], 0.0)
    for part in range(4):
        if part < 3:
            low, high = offsets_ref[part], cells_ref[part].astype(jnp.float32)
        else:
            low, high = power, jnp.zeros_like(power)
        own = jnp.concatenate([low, high], axis=1)
        far = jnp.concatenate([own[slabs // 2 :], own[: slabs // 2]], axis=0)
        for copy in range(rows // 8):
            sent_ref[pl.ds(copy * 8 + part, slabs, stride=rows), :] = own
            sent_ref[pl.ds(copy * 8 + 4 + part, slabs, stride=rows), :] = far


def partner(index, step, count):
    return index ^ step if count & (count - 1) == 0 else (index + step) % count


def spectrum_kernel(group, slabs, slab_ref, rows_ref, kx_ref, ky_ref, kappa_ref, near_ref, *rest):
    send_refs, (own_ref, far_ref, x_table_ref, y_table_ref, fine_table_ref) = (
        rest[:-5],
        rest[-5:],
    )
    kx_count = kx_ref.shape[0]
    ky_count = ky_ref.shape[0]
    blocks = rows_ref.shape[0] // 16
    kx, ky = kx_ref[...], ky_ref[...]
    kx_nodes, ky_nodes = node_phasors(kx), node_phasors(ky)
    row = lax.broadcasted_iota(jnp.int32, kx.shape, 0).astype(jnp.float32)
    key = jnp.abs(kx - jnp.round(kx)) * (NXD * kx_count) + row
    fine_masks, fine = [], []
    for _ in range(FINE):
        chosen = key == jnp.min(key, axis=0, keepdims=True)
        key = jnp.where(chosen, 2.0 * NXD * kx_count, key)
        fine_masks.append(jnp.where(chosen, 1.0, 0.0))
        fine.append(jnp.sum(jnp.where(chosen, kx, 0.0), axis=0, keepdims=True))
    fine_row = lax.broadcasted_iota(jnp.int32, (8, 128), 0)
    fine = jnp.where((fine_row & 1) == 0, fine[0], fine[1])
    fine_nodes = node_phasors(fine)
    columns = lax.broadcasted_iota(jnp.int32, (1, 128), 1).astype(jnp.float32)
    for freq, table_ref in ((kx, x_table_ref), (ky, y_table_ref), (fine, fine_table_ref)):
        table_ref[0], table_ref[1] = cos_sin_turns(freq * columns)
    low_lanes = lax.broadcasted_iota(jnp.int32, (8, 128), 1) < 64
    plane = lax.broadcasted_iota(jnp.int32, (40, 128), 0).astype(jnp.float32)

    def operands(frac, cell, column, side, weights, row):
        strength = frac[row + 3 : row + 4]
        base_z = cell[row : row + 1]
        column_x, column_y = column[row + 1 : row + 2], column[row + 2 : row + 3]
        side_x, side_y = side[row + 1 : row + 2], side[row + 2 : row + 3]
        wz = [w[row : row + 1] * strength for w in weights]
        wx = node_pairs([w[row + 1 : row + 2] for w in weights])
        wy = node_pairs([w[row + 2 : row + 3].astype(jnp.bfloat16).astype(jnp.float32) for w in weights])
        dist = plane - base_z
        spread = jnp.where(
            dist == 0.0,
            wz[0],
            jnp.where(dist == 1.0, wz[1], jnp.where(dist == 2.0, wz[2], jnp.where(dist == 3.0, wz[3], 0.0))),
        )
        cx, sx = transform(x_table_ref, kx_nodes, column_x, side_x, wx)
        cy, sy = transform(y_table_ref, ky_nodes, column_y, side_y, wy)
        lhs = []
        for z in range(PLANES):
            here = jnp.broadcast_to(spread[z : z + 1], cx.shape)
            lhs.append(
                jnp.concatenate([(here * cx).astype(jnp.bfloat16), (here * sx).astype(jnp.bfloat16)], axis=1)
            )
        if row == 0:
            fine_c, fine_s = transform(fine_table_ref, fine_nodes, column_x, side_x, wx)
            for z in range(0, spread.shape[0], 8):
                here = [
                    jnp.take_along_axis(spread[z : z + 8], (fine_row >> 1) + half, axis=0)
                    for half in range(0, 8, 8 // FINE)
                ]
                lhs.append(
                    jnp.concatenate(
                        [
                            two_parts(jnp.concatenate([h * part for h in here], axis=0))[1]
                            for part in (fine_c, fine_s)
                        ],
                        axis=1,
                    )
                )
        cy_high, cy_low = two_parts(cy)
        sy_high, sy_low = two_parts(-sy)
        rhs = [
            jnp.concatenate(pair, axis=1)
            for pair in ((cy_high, sy_high), (sy_high, -cy_high), (cy_low, sy_low), (sy_low, -cy_low))
        ]
        return jnp.concatenate(lhs, axis=0), jnp.concatenate(rhs, axis=0)

    def one_block(block):
        rows = rows_ref[pl.ds(pl.multiple_of(block * 16, 16), 16), :]
        turned = pltpu.roll(rows, 64, axis=1)
        frac = jnp.where(low_lanes, rows[0:8], turned[8:16])
        cell = jnp.where(low_lanes, turned[0:8], rows[8:16])
        weights = node_weights(frac)
        column = jnp.abs(cell - MIDDLE).astype(jnp.int32)
        side = jnp.where(cell < MIDDLE, -1.0, 1.0)
        return tuple(operands(frac, cell, column, side, weights, row) for row in (0, 4))

    def step(index, _):
        pieces = [one_block(index * group + j) for j in range(group)]
        for part, acc_ref in enumerate((own_ref, far_ref)):
            lhs = jnp.concatenate([p[part][0] for p in pieces], axis=1)
            rhs = jnp.concatenate([p[part][1] for p in pieces], axis=1)
            product = lax.dot_general(
                lhs, rhs, (((1,), (1,)), ((), ())), preferred_element_type=jnp.float32
            )

            @pl.when(index == 0)
            def _():
                acc_ref[...] = product

            @pl.when(index > 0)
            def _():
                acc_ref[...] += product

        return 0

    lax.fori_loop(0, blocks // group, step, 0)

    half = slabs // 2
    slab = slab_ref[0]
    upper = slab >= half
    first = jnp.where(upper, half, 0)
    member = slab - first
    far_slab = jnp.where(upper, slab - half, slab + half)
    kappa = kappa_ref[...]
    decay = jnp.exp(-kappa)
    width = 2 * ky_count

    def plane_of(acc_ref, z):
        start = z * kx_count
        both = acc_ref[pl.ds(start if isinstance(z, int) else pl.multiple_of(start, kx_count), kx_count), :]
        if acc_ref is own_ref:
            first = PLANES * kx_count + FINE * z
            for j, mask in enumerate(fine_masks):
                both_fine = acc_ref[first + j : first + j + 1, :]
                both = both + jnp.concatenate([mask, mask], axis=1) * both_fine
        return both[:, :width] + both[:, width:]

    def spills_of(acc_ref, index):
        inside = jnp.where(index < slabs - 1, 1.0, 0.0)
        return [plane_of(acc_ref, ZDEV + j) * inside for j in range(SPILL)]

    spilled = spills_of(own_ref, slab)
    down = spilled[0] + decay * (spilled[1] + decay * spilled[2])
    for z in range(ZDEV - 1, -1, -1):
        down = decay * down
        near_ref[z] = down
        down = plane_of(own_ref, z) + down
    up = jnp.zeros_like(decay)
    for z in range(ZDEV):
        up = plane_of(own_ref, z) + decay * up
        near_ref[z] += up
    up_near = spilled[0] + decay * up
    up_far = spilled[2] + decay * (spilled[1] + decay * up_near)

    far_spilled = spills_of(far_ref, far_slab)
    moment = jnp.where(
        upper, jnp.zeros_like(decay), far_spilled[0] + decay * (far_spilled[1] + decay * far_spilled[2])
    )
    for j in range(ZDEV):
        moment = plane_of(far_ref, jnp.where(upper, j, ZDEV - 1 - j)) + decay * moment
    far_near = far_spilled[0] + decay * moment
    far_far = far_spilled[2] + decay * (far_spilled[1] + decay * far_near)

    for hop, send_ref in enumerate(send_refs):
        target = first + partner(member, hop, half)
        zero = jnp.zeros_like(decay)
        ahead = target - slab
        reach = jnp.where(
            ahead > 1, ZDEV * ahead - (PLANES - 1), jnp.where(ahead < 0, ZDEV * (-ahead - 1), 0)
        )
        own_weight = jnp.exp(-kappa * reach.astype(jnp.float32))
        own_low = jnp.where(ahead > 0, own_weight * jnp.where(ahead == 1, up_near, up_far), zero)
        own_high = jnp.where(ahead < 0, own_weight * down, zero)
        far_ahead = target - far_slab
        far_reach = jnp.where(
            far_ahead > 1, ZDEV * far_ahead - (PLANES - 1), jnp.where(far_ahead < 0, ZDEV * (-far_ahead - 1), 0)
        )
        far_weight = jnp.exp(-kappa * far_reach.astype(jnp.float32))
        far_low = jnp.where(upper, far_weight * jnp.where(far_ahead == 1, far_near, far_far), zero)
        far_high = jnp.where(upper, zero, far_weight * moment)
        send_ref[0] = own_low + far_low
        send_ref[1] = own_high + far_high
        for j in (1, 2):
            send_ref[1 + j] = jnp.where(
                ahead == 1, spilled[j], jnp.where(far_ahead == 1, far_spilled[j], zero)
            )


def far_kernel(slabs, kappa_ref, turns_ref, near_ref, *rest):
    received_refs, out_ref, powers_ref = rest[:-2], rest[-2], rest[-1]
    kappa = kappa_ref[...]
    decay = jnp.exp(-kappa)
    sigma = 4.0 / (ZDEV * slabs)
    scale = (sigma * 2.0 / NXD) / kappa
    width = kappa.shape[1]
    turn_cos, turn_sin = cos_sin_turns(turns_ref[...])
    turn_cos = turn_cos * scale
    turn_sin = turn_sin * scale
    turn_sin = jnp.where(
        lax.broadcasted_iota(jnp.int32, kappa.shape, 1) < width // 2, turn_sin, -turn_sin
    )
    low, high, first, second = (sum(ref[part] for ref in received_refs) for part in range(4))
    for z in range(ZDEV - 1, -1, -1):
        high = decay * high
        powers_ref[z] = high
    extra = {0: decay * (first + decay * second), 1: decay * second}
    source_at = {1: first, 2: second}
    for z in range(ZDEV):
        if z:
            low = decay * low
        if z in source_at:
            low = low + source_at[z]
        total = near_ref[z] + low + powers_ref[z]
        if z in extra:
            total = total + extra[z]
        out_ref[z] = turn_cos * total + turn_sin * pltpu.roll(total, width // 2, axis=1)


def shards(offsets, strength, cells, counts, kx_modes, ky_modes):
    slabs = lax.axis_size("gz")
    x_groups = lax.axis_size("gx")
    half = slabs // 2
    cap = strength.shape[-1]
    slab = lax.axis_index("gz").astype(jnp.int32).reshape(1)

    smem = pl.BlockSpec(memory_space=pltpu.SMEM)
    vmem = pl.BlockSpec(memory_space=pltpu.VMEM)
    sent = pl.pallas_call(
        pack_kernel,
        out_shape=jax.ShapeDtypeStruct((slabs * x_groups * 8, 2 * cap), jnp.float32),
        in_specs=[smem, vmem, vmem, vmem],
        out_specs=vmem,
    )(counts, jnp.transpose(offsets[0], (1, 0, 2)), strength[0], jnp.transpose(cells[0], (1, 0, 2)))
    sent = sent.reshape(slabs * x_groups, 8, 2 * cap)
    arrived = lax.all_to_all(sent, ("gz", "gx"), split_axis=0, concat_axis=0, tiled=True)
    arrived = arrived.reshape(-1, 128)

    kx_local = kx_modes.shape[0] // x_groups
    ky_count = ky_modes.shape[0]
    own_kx = lax.dynamic_slice_in_dim(kx_modes, lax.axis_index("gx") * kx_local, kx_local)
    kx_turns = jnp.broadcast_to((own_kx.astype(jnp.float32) / NXD)[:, None], (kx_local, 128))
    ky_turns = jnp.broadcast_to((ky_modes.astype(jnp.float32) / NXD)[:, None], (ky_count, 128))
    signed_x = jnp.where(own_kx >= NXD // 2, own_kx - NXD, own_kx).astype(jnp.float32)
    signed_y = jnp.where(ky_modes >= NXD // 2, ky_modes - NXD, ky_modes).astype(jnp.float32)
    signed_y = jnp.concatenate([signed_y, signed_y])
    sigma = 4.0 / (ZDEV * slabs)
    step = 2.0 * math.pi / NXD
    kappa = jnp.sqrt(sigma * sigma + step * step * (signed_x[:, None] ** 2 + signed_y[None, :] ** 2))

    width = 2 * ky_count
    both_y = jnp.concatenate([ky_modes, ky_modes])
    turns = (own_kx[:, None] + both_y[None, :]).astype(jnp.float32) * ((MIDDLE + 1.5) / NXD)
    blocks = arrived.shape[0] // 16
    group = math.gcd(blocks, 16)
    planes = jax.ShapeDtypeStruct((ZDEV, kx_local, width), jnp.float32)
    message = jax.ShapeDtypeStruct((4, kx_local, width), jnp.float32)
    coarse_rows = PLANES * kx_local
    fine_rows = FINE * 8 * pl.cdiv(PLANES, 8)
    near, *messages = pl.pallas_call(
        functools.partial(spectrum_kernel, group, slabs),
        out_shape=(planes,) + (message,) * half,
        in_specs=[smem, vmem, vmem, vmem, vmem],
        out_specs=(vmem,) * (1 + half),
        scratch_shapes=[
            pltpu.VMEM((coarse_rows + fine_rows, 2 * width), jnp.float32),
            pltpu.VMEM((coarse_rows, 2 * width), jnp.float32),
            pltpu.VMEM((2, kx_local, 128), jnp.float32),
            pltpu.VMEM((2, ky_count, 128), jnp.float32),
            pltpu.VMEM((2, 8, 128), jnp.float32),
        ],
        compiler_params=pltpu.CompilerParams(vmem_limit_bytes=40 * 1024 * 1024),
    )(slab, arrived, kx_turns, ky_turns, kappa)

    received = messages[:1]
    for hop in range(1, half):
        pairs = [(i, i - i % half + partner(i % half, hop, half)) for i in range(slabs)]
        received.append(lax.ppermute(messages[hop], "gz", pairs))
    return pl.pallas_call(
        functools.partial(far_kernel, slabs),
        out_shape=planes,
        in_specs=[vmem] * (3 + half),
        out_specs=vmem,
        scratch_shapes=[pltpu.VMEM((ZDEV, kx_local, width), jnp.float32)],
        compiler_params=pltpu.CompilerParams(vmem_limit_bytes=32 * 1024 * 1024),
    )(kappa, turns, near, *received)


def solution(mesh):
    placed = (
        P("gx", "gz", None, None),
        P("gx", "gz", None),
        P("gx", "gz", None, None),
        P("gx", "gz"),
        P(),
        P(),
    )
    return jax.shard_map(
        shards, mesh=mesh, in_specs=placed, out_specs=P("gz", "gx", None), check_vma=False
    )
```

```python
import functools
import math

import jax
import jax.numpy as jnp
from jax import lax
from jax.experimental import pallas as pl
from jax.experimental.pallas import tpu as pltpu
from jax.sharding import PartitionSpec as P

NXD = 512
ZDEV = 32
SPILL = 3
PLANES = ZDEV + SPILL
MIDDLE = 126.0
FINE = 2

SIN_HALF = tuple(math.sqrt(2.0) * c for c in (3.14158202, -5.16714279, 2.54189899, -0.55463611))
COS_HALF = tuple(math.sqrt(2.0) * c for c in (0.9999933, -4.93393801, 4.04128375, -1.22212681))


def poly(u, coefs):
    total = jnp.full_like(u, coefs[-1])
    for c in coefs[-2::-1]:
        total = total * u + c
    return total


def cos_sin_turns(turns):
    r = turns - jnp.round(turns)
    u = r * r
    s = r * poly(u, SIN_HALF)
    return 1.0 - s * s, s * poly(u, COS_HALF)


def node_weights(f):
    g = 1.0 - f
    fg = -0.5 * f * g
    return (
        fg * g,
        1.0 + f * f * (1.5 * f - 2.5),
        1.0 + g * g * (1.5 * g - 2.5),
        fg * f,
    )


def node_phasors(freq):
    return cos_sin_turns(0.5 * freq) + cos_sin_turns(1.5 * freq)


def transform(table_ref, column, side, pairs):
    column = jnp.broadcast_to(column, table_ref.shape[1:])
    c = jnp.take_along_axis(table_ref[0], column, axis=1)
    s = jnp.take_along_axis(table_ref[1], column, axis=1) * side
    even1, odd1, even3, odd3 = pairs
    re = even1 * table_ref[2] + even3 * table_ref[4]
    im = odd1 * table_ref[3] + odd3 * table_ref[5]
    return c * re - s * im, s * re + c * im


def node_pairs(weights):
    w0, w1, w2, w3 = weights
    return w1 + w2, w2 - w1, w0 + w3, w3 - w0


def two_parts(x):
    high = x.astype(jnp.bfloat16)
    return high, (x - high.astype(jnp.float32)).astype(jnp.bfloat16)


def partner(index, step, count):
    return index ^ step if count & (count - 1) == 0 else (index + step) % count


def pack_rows(counts_ref, offsets_ref, strength_ref, cells_ref, sent_ref):
    slabs, cap = strength_ref.shape
    slot = lax.broadcasted_iota(jnp.int32, (slabs, cap), 0)
    lane = lax.broadcasted_iota(jnp.int32, (slabs, cap), 1)
    count = jnp.zeros((slabs, cap), jnp.int32)
    for d in range(slabs):
        count = jnp.where(slot == d, counts_ref[0, d], count)
    power = jnp.where(lane < count, strength_ref[...], 0.0)
    for part in range(4):
        if part < 3:
            low, high = offsets_ref[part], cells_ref[part].astype(jnp.float32)
        else:
            low, high = power, jnp.zeros_like(power)
        own = jnp.concatenate([low, high], axis=1)
        far = jnp.concatenate([own[slabs // 2 :], own[: slabs // 2]], axis=0)
        for first in range(0, sent_ref.shape[0], 8 * slabs):
            sent_ref[pl.ds(first + part, slabs, stride=8), :] = own
            sent_ref[pl.ds(first + 4 + part, slabs, stride=8), :] = far


def prepare_kernel(
    slabs, slab_ref, x_group_ref, counts_ref, offsets_ref, strength_ref, cells_ref, kx_modes_ref, ky_modes_ref,
    sent_ref, x_ref, y_ref, fine_ref, mask_ref, power_ref, weight_ref, turn_ref,
):
    pack_rows(counts_ref, offsets_ref, strength_ref, cells_ref, sent_ref)

    slab, x_group = slab_ref[0], x_group_ref[0]
    kx_count, ky_count = x_ref.shape[1], y_ref.shape[1]

    def down_rows(modes, rows, first):
        lane = lax.broadcasted_iota(jnp.int32, (rows, modes.shape[1]), 1)
        row = lax.broadcasted_iota(jnp.int32, (rows, modes.shape[1]), 0)
        picked = jnp.sum(jnp.where(lane == row + first, modes, 0.0), axis=1, keepdims=True)
        return jnp.broadcast_to(picked, (rows, 128))

    ky_modes = ky_modes_ref[...].astype(jnp.float32)
    kx_rows = down_rows(kx_modes_ref[...].astype(jnp.float32), kx_count, x_group * kx_count)
    ky_rows = down_rows(ky_modes, ky_count, 0)
    ky_lanes = jnp.concatenate([ky_modes, ky_modes], axis=1)
    kx, ky = kx_rows * (1.0 / NXD), ky_rows * (1.0 / NXD)
    sigma = 4.0 / (ZDEV * slabs)
    step = 2.0 * math.pi / NXD
    signed_x = jnp.where(kx_rows >= NXD // 2, kx_rows - NXD, kx_rows)
    signed_y = jnp.where(ky_lanes >= NXD // 2, ky_lanes - NXD, ky_lanes)
    kappa = jnp.sqrt(sigma * sigma + step * step * (signed_x * signed_x + signed_y * signed_y))
    turns = (kx_rows + ky_lanes) * ((MIDDLE + 1.5) / NXD)

    row = lax.broadcasted_iota(jnp.int32, kx.shape, 0).astype(jnp.float32)
    key = jnp.abs(kx - jnp.round(kx)) * (NXD * kx_count) + row
    fine = []
    for j in range(FINE):
        chosen = key == jnp.min(key, axis=0, keepdims=True)
        key = jnp.where(chosen, 2.0 * NXD * kx_count, key)
        mask_ref[j] = jnp.where(chosen, 1.0, 0.0)
        fine.append(jnp.sum(jnp.where(chosen, kx, 0.0), axis=0, keepdims=True))
    fine_row = lax.broadcasted_iota(jnp.int32, (8, 128), 0)
    fine = jnp.where((fine_row & 1) == 0, fine[0], fine[1])

    columns = lax.broadcasted_iota(jnp.int32, (1, 128), 1).astype(jnp.float32)
    for freq, table_ref in ((kx, x_ref), (ky, y_ref), (fine, fine_ref)):
        for j, part in enumerate(cos_sin_turns(freq * columns) + node_phasors(freq)):
            table_ref[j] = part

    decay = jnp.exp(-kappa)
    power = jnp.ones_like(kappa)
    for z in range(ZDEV + 1):
        power_ref[z] = power
        power = power * decay

    half = slabs // 2
    first = jnp.where(slab >= half, half, 0)
    far_slab = jnp.where(slab >= half, slab - half, slab + half)
    for hop in range(half):
        target = first + partner(slab - first, hop, half)
        for j, source in enumerate((slab, far_slab)):
            ahead = target - source
            reach = jnp.where(
                ahead > 1, ZDEV * ahead - (PLANES - 1), jnp.where(ahead < 0, ZDEV * (-ahead - 1), 0)
            )
            weight_ref[2 * hop + j] = jnp.exp(-kappa * reach.astype(jnp.float32))

    scale = (sigma * 2.0 / NXD) / kappa
    turn_cos, turn_sin = cos_sin_turns(turns)
    real = lax.broadcasted_iota(jnp.int32, kappa.shape, 1) < kappa.shape[1] // 2
    turn_ref[0] = scale * turn_cos
    turn_ref[1] = scale * jnp.where(real, turn_sin, -turn_sin)


def spectrum_kernel(
    group, slabs, slab_ref, rows_ref, x_ref, y_ref, fine_ref, mask_ref, power_ref, weight_ref, near_ref, *rest
):
    send_refs, (own_ref, far_ref) = rest[:-2], rest[-2:]
    kx_count = x_ref.shape[1]
    ky_count = y_ref.shape[1]
    blocks = rows_ref.shape[0] // 16
    low_lanes = lax.broadcasted_iota(jnp.int32, (8, 128), 1) < 64
    plane = lax.broadcasted_iota(jnp.int32, (40, 128), 0).astype(jnp.float32)
    fine_row = lax.broadcasted_iota(jnp.int32, (8, 128), 0)

    def operands(frac, cell, column, side, weights, row):
        strength = frac[row + 3 : row + 4]
        base_z = cell[row : row + 1]
        column_x, column_y = column[row + 1 : row + 2], column[row + 2 : row + 3]
        side_x, side_y = side[row + 1 : row + 2], side[row + 2 : row + 3]
        wz = [w[row : row + 1] * strength for w in weights]
        wx = node_pairs([w[row + 1 : row + 2] for w in weights])
        wy = node_pairs([w[row + 2 : row + 3].astype(jnp.bfloat16).astype(jnp.float32) for w in weights])
        dist = plane - base_z
        spread = jnp.where(
            dist == 0.0,
            wz[0],
            jnp.where(dist == 1.0, wz[1], jnp.where(dist == 2.0, wz[2], jnp.where(dist == 3.0, wz[3], 0.0))),
        )
        cx, sx = transform(x_ref, column_x, side_x, wx)
        cy, sy = transform(y_ref, column_y, side_y, wy)
        lhs = []
        for z in range(PLANES):
            here = jnp.broadcast_to(spread[z : z + 1], cx.shape)
            lhs.append(
                jnp.concatenate([(here * cx).astype(jnp.bfloat16), (here * sx).astype(jnp.bfloat16)], axis=1)
            )
        if row == 0:
            fine_c, fine_s = transform(fine_ref, column_x, side_x, wx)
            for z in range(0, spread.shape[0], 8):
                here = [
                    jnp.take_along_axis(spread[z : z + 8], (fine_row >> 1) + half, axis=0)
                    for half in range(0, 8, 8 // FINE)
                ]
                lhs.append(
                    jnp.concatenate(
                        [
                            two_parts(jnp.concatenate([h * part for h in here], axis=0))[1]
                            for part in (fine_c, fine_s)
                        ],
                        axis=1,
                    )
                )
        cy_high, cy_low = two_parts(cy)
        sy_high, sy_low = two_parts(-sy)
        rhs = [
            jnp.concatenate(pair, axis=1)
            for pair in ((cy_high, sy_high), (sy_high, -cy_high), (cy_low, sy_low), (sy_low, -cy_low))
        ]
        return jnp.concatenate(lhs, axis=0), jnp.concatenate(rhs, axis=0)

    def one_block(block):
        rows = rows_ref[pl.ds(pl.multiple_of(block * 16, 16), 16), :]
        turned = pltpu.roll(rows, 64, axis=1)
        frac = jnp.where(low_lanes, rows[0:8], turned[8:16])
        cell = jnp.where(low_lanes, turned[0:8], rows[8:16])
        weights = node_weights(frac)
        column = jnp.abs(cell - MIDDLE).astype(jnp.int32)
        side = jnp.where(cell < MIDDLE, -1.0, 1.0)
        return tuple(operands(frac, cell, column, side, weights, row) for row in (0, 4))

    def step(index, _):
        pieces = [one_block(index * group + j) for j in range(group)]
        for part, acc_ref in enumerate((own_ref, far_ref)):
            lhs = jnp.concatenate([p[part][0] for p in pieces], axis=1)
            rhs = jnp.concatenate([p[part][1] for p in pieces], axis=1)
            product = lax.dot_general(
                lhs, rhs, (((1,), (1,)), ((), ())), preferred_element_type=jnp.float32
            )

            @pl.when(index == 0)
            def _():
                acc_ref[...] = product

            @pl.when(index > 0)
            def _():
                acc_ref[...] += product

        return 0

    lax.fori_loop(0, blocks // group, step, 0)

    half = slabs // 2
    slab = slab_ref[0]
    upper = slab >= half
    first = jnp.where(upper, half, 0)
    member = slab - first
    far_slab = jnp.where(upper, slab - half, slab + half)
    decay = power_ref[1]
    width = 2 * ky_count

    def plane_of(acc_ref, z):
        start = z * kx_count
        both = acc_ref[pl.ds(start if isinstance(z, int) else pl.multiple_of(start, kx_count), kx_count), :]
        plane = both[:, :width] + both[:, width:]
        if acc_ref is own_ref:
            first = PLANES * kx_count + FINE * z
            for j in range(FINE):
                plane = plane + mask_ref[j] * acc_ref[first + j : first + j + 1, :width]
        return plane

    def spills_of(acc_ref, index):
        inside = jnp.where(index < slabs - 1, 1.0, 0.0)
        return [plane_of(acc_ref, ZDEV + j) * inside for j in range(SPILL)]

    spilled = spills_of(own_ref, slab)
    down = spilled[0] + decay * (spilled[1] + decay * spilled[2])
    for z in range(ZDEV - 1, -1, -1):
        down = decay * down
        near_ref[z] = down
        down = plane_of(own_ref, z) + down
    up = jnp.zeros_like(decay)
    for z in range(ZDEV):
        up = plane_of(own_ref, z) + decay * up
        near_ref[z] += up
    up_near = spilled[0] + decay * up
    up_far = spilled[2] + decay * (spilled[1] + decay * up_near)

    far_spilled = spills_of(far_ref, far_slab)
    moment = jnp.where(
        upper, jnp.zeros_like(decay), far_spilled[0] + decay * (far_spilled[1] + decay * far_spilled[2])
    )
    for j in range(ZDEV):
        moment = plane_of(far_ref, jnp.where(upper, j, ZDEV - 1 - j)) + decay * moment
    far_near = far_spilled[0] + decay * moment
    far_far = far_spilled[2] + decay * (far_spilled[1] + decay * far_near)

    for hop, send_ref in enumerate(send_refs):
        target = first + partner(member, hop, half)
        zero = jnp.zeros_like(decay)
        ahead = target - slab
        own_weight = weight_ref[2 * hop]
        own_low = jnp.where(ahead > 0, own_weight * jnp.where(ahead == 1, up_near, up_far), zero)
        own_high = jnp.where(ahead < 0, own_weight * down, zero)
        far_ahead = target - far_slab
        far_weight = weight_ref[2 * hop + 1]
        far_low = jnp.where(upper, far_weight * jnp.where(far_ahead == 1, far_near, far_far), zero)
        far_high = jnp.where(upper, zero, far_weight * moment)
        send_ref[0] = own_low + far_low
        send_ref[1] = own_high + far_high
        for j in (1, 2):
            send_ref[1 + j] = jnp.where(
                ahead == 1, spilled[j], jnp.where(far_ahead == 1, far_spilled[j], zero)
            )


def far_kernel(power_ref, turn_ref, near_ref, *rest):
    received_refs, out_ref = rest[:-1], rest[-1]
    low, high, first, second = (sum(ref[part] for ref in received_refs) for part in range(4))
    decay = power_ref[1]
    turn_cos, turn_sin = turn_ref[0], turn_ref[1]
    low_at = [
        low + decay * (first + decay * second),
        decay * low + first + decay * second,
        decay * (decay * low + first) + second,
    ]
    for z in range(ZDEV):
        total = near_ref[z] + power_ref[ZDEV - z] * high
        total = total + (low_at[z] if z < 3 else power_ref[z - 2] * low_at[2])
        out_ref[z] = turn_cos * total + turn_sin * pltpu.roll(total, total.shape[1] // 2, axis=1)


def shards(offsets, strength, cells, counts, kx_modes, ky_modes):
    slabs = lax.axis_size("gz")
    x_groups = lax.axis_size("gx")
    half = slabs // 2
    cap = strength.shape[-1]
    kx_local = kx_modes.shape[0] // x_groups
    ky_count = ky_modes.shape[0]
    width = 2 * ky_count
    slab = lax.axis_index("gz").astype(jnp.int32).reshape(1)
    x_group = lax.axis_index("gx").astype(jnp.int32).reshape(1)

    smem = pl.BlockSpec(memory_space=pltpu.SMEM)
    vmem = pl.BlockSpec(memory_space=pltpu.VMEM)
    some = 16 * 1024 * 1024

    def shaped(*shape):
        return jax.ShapeDtypeStruct(shape, jnp.float32)

    prepared = (
        shaped(slabs * x_groups * 8, 2 * cap),
        shaped(6, kx_local, 128),
        shaped(6, ky_count, 128),
        shaped(6, 8, 128),
        shaped(FINE, kx_local, width),
        shaped(ZDEV + 1, kx_local, width),
        shaped(2 * half, kx_local, width),
        shaped(2, kx_local, width),
    )
    inputs = (
        jnp.transpose(offsets[0], (1, 0, 2)),
        strength[0],
        jnp.transpose(cells[0], (1, 0, 2)),
        kx_modes.reshape(1, -1),
        ky_modes.reshape(1, -1),
    )
    sent, *tables, turn = pl.pallas_call(
        functools.partial(prepare_kernel, slabs),
        out_shape=prepared,
        in_specs=[smem] * 3 + [vmem] * len(inputs),
        out_specs=(vmem,) * len(prepared),
        compiler_params=pltpu.CompilerParams(vmem_limit_bytes=some),
    )(slab, x_group, *(pltpu.with_memory_space_constraint(array, pltpu.HBM) for array in (counts,) + inputs))
    powers = tables[4]
    sent = sent.reshape(slabs * x_groups, 8, 2 * cap)
    arrived = lax.all_to_all(sent, ("gx", "gz"), split_axis=0, concat_axis=0, tiled=True)
    arrived = arrived.reshape(-1, 128)

    blocks = arrived.shape[0] // 16
    group = math.gcd(blocks, 16)
    planes = shaped(ZDEV, kx_local, width)
    message = shaped(4, kx_local, width)
    coarse_rows = PLANES * kx_local
    fine_rows = FINE * 8 * pl.cdiv(PLANES, 8)
    near, *messages = pl.pallas_call(
        functools.partial(spectrum_kernel, group, slabs),
        out_shape=(planes,) + (message,) * half,
        in_specs=[smem] + [vmem] * (1 + len(tables)),
        out_specs=(vmem,) * (1 + half),
        scratch_shapes=[
            pltpu.VMEM((coarse_rows + fine_rows, 2 * width), jnp.float32),
            pltpu.VMEM((coarse_rows, 2 * width), jnp.float32),
        ],
        compiler_params=pltpu.CompilerParams(vmem_limit_bytes=40 * 1024 * 1024),
    )(slab, arrived, *tables)

    received = messages[:1]
    for hop in range(1, half):
        pairs = [(i, i - i % half + partner(i % half, hop, half)) for i in range(slabs)]
        received.append(lax.ppermute(messages[hop], "gz", pairs))
    return pl.pallas_call(
        far_kernel,
        out_shape=planes,
        in_specs=[vmem] * (3 + half),
        out_specs=vmem,
        compiler_params=pltpu.CompilerParams(vmem_limit_bytes=some),
    )(powers, turn, near, *received)


def solution(mesh):
    placed = (
        P("gx", "gz", None, None),
        P("gx", "gz", None),
        P("gx", "gz", None, None),
        P("gx", "gz"),
        P(),
        P(),
    )
    return jax.shard_map(
        shards, mesh=mesh, in_specs=placed, out_specs=P("gz", "gx", None), check_vma=False
    )
```

```python
import functools
import math

import jax
import jax.numpy as jnp
from jax import lax
from jax.experimental import pallas as pl
from jax.experimental.pallas import tpu as pltpu
from jax.sharding import PartitionSpec as P

NXD = 512
ZDEV = 32
SPILL = 3
PLANES = ZDEV + SPILL
MIDDLE = 126.0
FINE = 2

SIN_HALF = tuple(math.sqrt(2.0) * c for c in (3.14158202, -5.16714279, 2.54189899, -0.55463611))
COS_HALF = tuple(math.sqrt(2.0) * c for c in (0.9999933, -4.93393801, 4.04128375, -1.22212681))


def poly(u, coefs):
    total = jnp.full_like(u, coefs[-1])
    for c in coefs[-2::-1]:
        total = total * u + c
    return total


def cos_sin_turns(turns):
    r = turns - jnp.round(turns)
    u = r * r
    s = r * poly(u, SIN_HALF)
    return 1.0 - s * s, s * poly(u, COS_HALF)


def node_weights(f):
    g = 1.0 - f
    fg = -0.5 * f * g
    return (
        fg * g,
        1.0 + f * f * (1.5 * f - 2.5),
        1.0 + g * g * (1.5 * g - 2.5),
        fg * f,
    )


def node_phasors(freq):
    return cos_sin_turns(0.5 * freq) + cos_sin_turns(1.5 * freq)


def transform(table_ref, column, side, pairs):
    column = jnp.broadcast_to(column, table_ref.shape[1:])
    c = jnp.take_along_axis(table_ref[0], column, axis=1)
    s = jnp.take_along_axis(table_ref[1], column, axis=1) * side
    even1, odd1, even3, odd3 = pairs
    re = even1 * table_ref[2] + even3 * table_ref[4]
    im = odd1 * table_ref[3] + odd3 * table_ref[5]
    return c * re - s * im, s * re + c * im


def node_pairs(weights):
    w0, w1, w2, w3 = weights
    return w1 + w2, w2 - w1, w0 + w3, w3 - w0


def two_parts(x):
    high = x.astype(jnp.bfloat16)
    return high, (x - high.astype(jnp.float32)).astype(jnp.bfloat16)


def partner(index, step, count):
    return index ^ step if count & (count - 1) == 0 else (index + step) % count


def pack_rows(counts_ref, offsets_ref, strength_ref, cells_ref, sent_ref):
    slabs, cap = strength_ref.shape
    slot = lax.broadcasted_iota(jnp.int32, (slabs, cap), 0)
    lane = lax.broadcasted_iota(jnp.int32, (slabs, cap), 1)
    count = jnp.zeros((slabs, cap), jnp.int32)
    for d in range(slabs):
        count = jnp.where(slot == d, counts_ref[0, d], count)
    power = jnp.where(lane < count, strength_ref[...], 0.0)
    for part in range(4):
        if part < 3:
            low, high = offsets_ref[part], cells_ref[part].astype(jnp.float32)
        else:
            low, high = power, jnp.zeros_like(power)
        own = jnp.concatenate([low, high], axis=1)
        far = jnp.concatenate([own[slabs // 2 :], own[: slabs // 2]], axis=0)
        for first in range(0, sent_ref.shape[0], 8 * slabs):
            sent_ref[pl.ds(first + part, slabs, stride=8), :] = own
            sent_ref[pl.ds(first + 4 + part, slabs, stride=8), :] = far


def prepare_kernel(
    slabs, slab_ref, x_group_ref, counts_ref, offsets_ref, strength_ref, cells_ref, kx_modes_ref, ky_modes_ref,
    sent_ref, x_ref, y_ref, fine_ref, mask_ref, power_ref, weight_ref, turn_ref,
):
    pack_rows(counts_ref, offsets_ref, strength_ref, cells_ref, sent_ref)

    slab, x_group = slab_ref[0], x_group_ref[0]
    kx_count, ky_count = x_ref.shape[1], y_ref.shape[1]

    def down_rows(modes, rows, first):
        lane = lax.broadcasted_iota(jnp.int32, (rows, modes.shape[1]), 1)
        row = lax.broadcasted_iota(jnp.int32, (rows, modes.shape[1]), 0)
        picked = jnp.sum(jnp.where(lane == row + first, modes, 0.0), axis=1, keepdims=True)
        return jnp.broadcast_to(picked, (rows, 128))

    ky_modes = ky_modes_ref[...].astype(jnp.float32)
    kx_rows = down_rows(kx_modes_ref[...].astype(jnp.float32), kx_count, x_group * kx_count)
    ky_rows = down_rows(ky_modes, ky_count, 0)
    ky_lanes = jnp.concatenate([ky_modes, ky_modes], axis=1)
    kx, ky = kx_rows * (1.0 / NXD), ky_rows * (1.0 / NXD)
    sigma = 4.0 / (ZDEV * slabs)
    step = 2.0 * math.pi / NXD
    signed_x = jnp.where(kx_rows >= NXD // 2, kx_rows - NXD, kx_rows)
    signed_y = jnp.where(ky_lanes >= NXD // 2, ky_lanes - NXD, ky_lanes)
    kappa = jnp.sqrt(sigma * sigma + step * step * (signed_x * signed_x + signed_y * signed_y))
    turns = (kx_rows + ky_lanes) * ((MIDDLE + 1.5) / NXD)

    row = lax.broadcasted_iota(jnp.int32, kx.shape, 0).astype(jnp.float32)
    key = jnp.abs(kx - jnp.round(kx)) * (NXD * kx_count) + row
    fine = []
    for j in range(FINE):
        chosen = key == jnp.min(key, axis=0, keepdims=True)
        key = jnp.where(chosen, 2.0 * NXD * kx_count, key)
        mask_ref[j] = jnp.where(chosen, 1.0, 0.0)
        fine.append(jnp.sum(jnp.where(chosen, kx, 0.0), axis=0, keepdims=True))
    fine_row = lax.broadcasted_iota(jnp.int32, (8, 128), 0)
    fine = jnp.where((fine_row & 1) == 0, fine[0], fine[1])

    columns = lax.broadcasted_iota(jnp.int32, (1, 128), 1).astype(jnp.float32)
    for freq, table_ref in ((kx, x_ref), (ky, y_ref), (fine, fine_ref)):
        for j, part in enumerate(cos_sin_turns(freq * columns) + node_phasors(freq)):
            table_ref[j] = part

    decay = jnp.exp(-kappa)
    power = jnp.ones_like(kappa)
    for z in range(ZDEV + 1):
        power_ref[z] = power
        power = power * decay

    half = slabs // 2
    first = jnp.where(slab >= half, half, 0)
    far_slab = jnp.where(slab >= half, slab - half, slab + half)
    for hop in range(half):
        target = first + partner(slab - first, hop, half)
        for j, source in enumerate((slab, far_slab)):
            ahead = target - source
            reach = jnp.where(
                ahead > 1, ZDEV * ahead - (PLANES - 1), jnp.where(ahead < 0, ZDEV * (-ahead - 1), 0)
            )
            weight = jnp.exp(-kappa * reach.astype(jnp.float32))
            for k, joins in enumerate((ahead == 1, ahead > 1, ahead < 0)):
                weight_ref[6 * hop + 3 * j + k] = jnp.where(joins, weight, 0.0)
    for j, source in enumerate((slab, far_slab)):
        weight_ref[6 * half + j] = jnp.full(kappa.shape, jnp.where(source < slabs - 1, 1.0, 0.0))

    scale = (sigma * 2.0 / NXD) / kappa
    turn_cos, turn_sin = cos_sin_turns(turns)
    real = lax.broadcasted_iota(jnp.int32, kappa.shape, 1) < kappa.shape[1] // 2
    turn_ref[0] = scale * turn_cos
    turn_ref[1] = scale * jnp.where(real, turn_sin, -turn_sin)


def spectrum_kernel(
    group, joined, rows_ref, x_ref, y_ref, fine_ref, mask_ref, power_ref, weight_ref, near_ref, *rest
):
    send_refs, (own_ref, far_ref) = rest[:-2], rest[-2:]
    kx_count = x_ref.shape[1]
    ky_count = y_ref.shape[1]
    blocks = rows_ref.shape[0] // 16
    low_lanes = lax.broadcasted_iota(jnp.int32, (8, 128), 1) < 64
    plane = lax.broadcasted_iota(jnp.int32, (40, 128), 0).astype(jnp.float32)
    fine_row = lax.broadcasted_iota(jnp.int32, (8, 128), 0)

    def operands(frac, cell, column, side, weights, row):
        strength = frac[row + 3 : row + 4]
        base_z = cell[row : row + 1]
        column_x, column_y = column[row + 1 : row + 2], column[row + 2 : row + 3]
        side_x, side_y = side[row + 1 : row + 2], side[row + 2 : row + 3]
        wz = [w[row : row + 1] * strength for w in weights]
        wx = node_pairs([w[row + 1 : row + 2] for w in weights])
        wy = node_pairs([w[row + 2 : row + 3].astype(jnp.bfloat16).astype(jnp.float32) for w in weights])
        dist = plane - base_z
        spread = jnp.where(
            dist == 0.0,
            wz[0],
            jnp.where(dist == 1.0, wz[1], jnp.where(dist == 2.0, wz[2], jnp.where(dist == 3.0, wz[3], 0.0))),
        )
        cx, sx = transform(x_ref, column_x, side_x, wx)
        cy, sy = transform(y_ref, column_y, side_y, wy)
        lhs = []
        for z in range(PLANES):
            here = jnp.broadcast_to(spread[z : z + 1], cx.shape)
            lhs.append(
                jnp.concatenate([(here * cx).astype(jnp.bfloat16), (here * sx).astype(jnp.bfloat16)], axis=1)
            )
        if row == 0:
            fine_c, fine_s = transform(fine_ref, column_x, side_x, wx)
            for z in range(0, spread.shape[0], 8):
                here = [
                    jnp.take_along_axis(spread[z : z + 8], (fine_row >> 1) + half, axis=0)
                    for half in range(0, 8, 8 // FINE)
                ]
                lhs.append(
                    jnp.concatenate(
                        [
                            two_parts(jnp.concatenate([h * part for h in here], axis=0))[1]
                            for part in (fine_c, fine_s)
                        ],
                        axis=1,
                    )
                )
        cy_high, cy_low = two_parts(cy)
        sy_high, sy_low = two_parts(-sy)
        rhs = [
            jnp.concatenate(pair, axis=1)
            for pair in ((cy_high, sy_high), (sy_high, -cy_high), (cy_low, sy_low), (sy_low, -cy_low))
        ]
        return jnp.concatenate(lhs, axis=0), jnp.concatenate(rhs, axis=0)

    def one_block(block):
        rows = rows_ref[pl.ds(pl.multiple_of(block * 16, 16), 16), :]
        turned = pltpu.roll(rows, 64, axis=1)
        frac = jnp.where(low_lanes, rows[0:8], turned[8:16])
        cell = jnp.where(low_lanes, turned[0:8], rows[8:16])
        weights = node_weights(frac)
        column = jnp.abs(cell - MIDDLE).astype(jnp.int32)
        side = jnp.where(cell < MIDDLE, -1.0, 1.0)
        return tuple(operands(frac, cell, column, side, weights, row) for row in (0, 4))

    def step(index, _):
        pieces = [one_block(index * group + j) for j in range(group)]
        for part, acc_ref in enumerate((own_ref, far_ref)):
            lhs = jnp.concatenate([p[part][0] for p in pieces], axis=1)
            rhs = jnp.concatenate([p[part][1] for p in pieces], axis=1)
            product = lax.dot_general(
                lhs, rhs, (((1,), (1,)), ((), ())), preferred_element_type=jnp.float32
            )

            @pl.when(index == 0)
            def _():
                acc_ref[...] = product

            @pl.when(index > 0)
            def _():
                acc_ref[...] += product

        return 0

    lax.fori_loop(0, blocks // group, step, 0)

    decay = power_ref[1]
    width = 2 * ky_count

    def plane_of(acc_ref, z):
        both = acc_ref[z * kx_count : (z + 1) * kx_count, :]
        plane = both[:, :width] + both[:, width:]
        if acc_ref is own_ref:
            first = PLANES * kx_count + FINE * z
            for j in range(FINE):
                plane = plane + mask_ref[j] * acc_ref[first + j : first + j + 1, :width]
        return plane

    parts = []
    for j, acc_ref in enumerate((own_ref, far_ref)):
        inside = weight_ref[6 * len(send_refs) + j]
        spilled = [plane_of(acc_ref, ZDEV + k) * inside for k in range(SPILL)]
        down = spilled[0] + decay * (spilled[1] + decay * spilled[2])
        for z in range(ZDEV - 1, -1, -1):
            down = decay * down
            if j == 0:
                near_ref[z] = down
            down = plane_of(acc_ref, z) + down
        up = jnp.zeros_like(decay)
        for z in range(ZDEV):
            up = plane_of(acc_ref, z) + decay * up
            if j == 0:
                near_ref[z] += up
        up_near = spilled[0] + decay * up
        up_far = spilled[2] + decay * (spilled[1] + decay * up_near)
        parts.append((spilled, up_near, up_far, down))

    for hop, send_ref in enumerate(send_refs):
        low = high = first = second = 0.0
        for j, (spilled, up_near, up_far, down) in enumerate(parts):
            near_above, above, below = (weight_ref[6 * hop + 3 * j + k] for k in range(3))
            low = low + above * up_far
            high = high + below * down
            if joined[hop]:
                low = low + near_above * up_near
                first = first + near_above * spilled[1]
                second = second + near_above * spilled[2]
        send_ref[0] = low
        send_ref[1] = high
        if joined[hop]:
            send_ref[2] = first
            send_ref[3] = second


def far_kernel(power_ref, turn_ref, near_ref, *rest):
    received_refs, out_ref = rest[:-1], rest[-1]
    low, high, first, second = (
        sum(ref[part] for ref in received_refs if part < ref.shape[0]) for part in range(4)
    )
    decay = power_ref[1]
    turn_cos, turn_sin = turn_ref[0], turn_ref[1]
    low_at = [
        low + decay * (first + decay * second),
        decay * low + first + decay * second,
        decay * (decay * low + first) + second,
    ]
    for z in range(ZDEV):
        total = near_ref[z] + power_ref[ZDEV - z] * high
        total = total + (low_at[z] if z < 3 else power_ref[z - 2] * low_at[2])
        out_ref[z] = turn_cos * total + turn_sin * pltpu.roll(total, total.shape[1] // 2, axis=1)


def shards(offsets, strength, cells, counts, kx_modes, ky_modes):
    slabs = lax.axis_size("gz")
    x_groups = lax.axis_size("gx")
    half = slabs // 2
    cap = strength.shape[-1]
    kx_local = kx_modes.shape[0] // x_groups
    ky_count = ky_modes.shape[0]
    width = 2 * ky_count
    slab = lax.axis_index("gz").astype(jnp.int32).reshape(1)
    x_group = lax.axis_index("gx").astype(jnp.int32).reshape(1)

    smem = pl.BlockSpec(memory_space=pltpu.SMEM)
    vmem = pl.BlockSpec(memory_space=pltpu.VMEM)
    some = 16 * 1024 * 1024

    def shaped(*shape):
        return jax.ShapeDtypeStruct(shape, jnp.float32)

    prepared = (
        shaped(slabs * x_groups * 8, 2 * cap),
        shaped(6, kx_local, 128),
        shaped(6, ky_count, 128),
        shaped(6, 8, 128),
        shaped(FINE, kx_local, width),
        shaped(ZDEV + 1, kx_local, width),
        shaped(6 * half + 2, kx_local, width),
        shaped(2, kx_local, width),
    )
    inputs = (
        jnp.transpose(offsets[0], (1, 0, 2)),
        strength[0],
        jnp.transpose(cells[0], (1, 0, 2)),
        kx_modes.reshape(1, -1),
        ky_modes.reshape(1, -1),
    )
    sent, *tables, turn = pl.pallas_call(
        functools.partial(prepare_kernel, slabs),
        out_shape=prepared,
        in_specs=[smem] * 3 + [vmem] * len(inputs),
        out_specs=(vmem,) * len(prepared),
        compiler_params=pltpu.CompilerParams(vmem_limit_bytes=some),
    )(slab, x_group, *(pltpu.with_memory_space_constraint(array, pltpu.HBM) for array in (counts,) + inputs))
    powers = tables[4]
    sent = sent.reshape(slabs * x_groups, 8, 2 * cap)
    arrived = lax.all_to_all(sent, ("gx", "gz"), split_axis=0, concat_axis=0, tiled=True)
    arrived = arrived.reshape(-1, 128)

    blocks = arrived.shape[0] // 16
    group = math.gcd(blocks, 16)
    planes = shaped(ZDEV, kx_local, width)
    joined = [
        any(partner(m, hop, half) == (m + 1) % half for m in range(half)) for hop in range(half)
    ]
    coarse_rows = PLANES * kx_local
    fine_rows = FINE * 8 * pl.cdiv(PLANES, 8)
    near, *messages = pl.pallas_call(
        functools.partial(spectrum_kernel, group, joined),
        out_shape=(planes,) + tuple(shaped(4 if joins else 2, kx_local, width) for joins in joined),
        in_specs=[vmem] * (1 + len(tables)),
        out_specs=(vmem,) * (1 + half),
        scratch_shapes=[
            pltpu.VMEM((coarse_rows + fine_rows, 2 * width), jnp.float32),
            pltpu.VMEM((coarse_rows, 2 * width), jnp.float32),
        ],
        compiler_params=pltpu.CompilerParams(vmem_limit_bytes=40 * 1024 * 1024),
    )(arrived, *tables)

    received = messages[:1]
    for hop in range(1, half):
        pairs = [(i, i - i % half + partner(i % half, hop, half)) for i in range(slabs)]
        received.append(lax.ppermute(messages[hop], "gz", pairs))
    return pl.pallas_call(
        far_kernel,
        out_shape=planes,
        in_specs=[vmem] * (3 + half),
        out_specs=vmem,
        compiler_params=pltpu.CompilerParams(vmem_limit_bytes=some),
    )(powers, turn, near, *received)


def solution(mesh):
    placed = (
        P("gx", "gz", None, None),
        P("gx", "gz", None),
        P("gx", "gz", None, None),
        P("gx", "gz"),
        P(),
        P(),
    )
    return jax.shard_map(
        shards, mesh=mesh, in_specs=placed, out_specs=P("gz", "gx", None), check_vma=False
    )
```

```python
import functools
import math

import jax
import jax.numpy as jnp
from jax import lax
from jax.experimental import pallas as pl
from jax.experimental.pallas import tpu as pltpu
from jax.sharding import PartitionSpec as P

NXD = 512
ZDEV = 32
SPILL = 3
PLANES = ZDEV + SPILL
MIDDLE = 126.0
FINE = 2

SIN_HALF = tuple(math.sqrt(2.0) * c for c in (3.14158202, -5.16714279, 2.54189899, -0.55463611))
COS_HALF = tuple(math.sqrt(2.0) * c for c in (0.9999933, -4.93393801, 4.04128375, -1.22212681))


def poly(u, coefs):
    total = jnp.full_like(u, coefs[-1])
    for c in coefs[-2::-1]:
        total = total * u + c
    return total


def cos_sin_turns(turns):
    r = turns - jnp.round(turns)
    u = r * r
    s = r * poly(u, SIN_HALF)
    return 1.0 - s * s, s * poly(u, COS_HALF)


def node_weights(f):
    g = 1.0 - f
    fg = -0.5 * f * g
    return (
        fg * g,
        1.0 + f * f * (1.5 * f - 2.5),
        1.0 + g * g * (1.5 * g - 2.5),
        fg * f,
    )


def node_phasors(freq):
    return cos_sin_turns(0.5 * freq) + cos_sin_turns(1.5 * freq)


def lookup(table_ref, column, side):
    column = jnp.broadcast_to(column, table_ref.shape[1:])
    c = jnp.take_along_axis(table_ref[0], column, axis=1)
    return c, jnp.take_along_axis(table_ref[1], column, axis=1) * side


def turned(c, s, table_ref, pairs):
    even1, odd1, even3, odd3 = pairs
    re = even1 * table_ref[2] + even3 * table_ref[4]
    im = odd1 * table_ref[3] + odd3 * table_ref[5]
    return c * re - s * im, s * re + c * im


def transform(table_ref, column, side, pairs):
    return turned(*lookup(table_ref, column, side), table_ref, pairs)


def node_pairs(weights):
    w0, w1, w2, w3 = weights
    return w1 + w2, w2 - w1, w0 + w3, w3 - w0


def two_parts(x):
    high = x.astype(jnp.bfloat16)
    return high, (x - high.astype(jnp.float32)).astype(jnp.bfloat16)


def partner(index, step, count):
    return index ^ step if count & (count - 1) == 0 else (index + step) % count


def pack_rows(counts_ref, offsets_ref, strength_ref, cells_ref, sent_ref):
    slabs, cap = strength_ref.shape
    slot = lax.broadcasted_iota(jnp.int32, (slabs, cap), 0)
    lane = lax.broadcasted_iota(jnp.int32, (slabs, cap), 1)
    count = jnp.zeros((slabs, cap), jnp.int32)
    for d in range(slabs):
        count = jnp.where(slot == d, counts_ref[0, d], count)
    power = jnp.where(lane < count, strength_ref[...], 0.0)
    for part in range(4):
        if part < 3:
            low, high = offsets_ref[part], cells_ref[part].astype(jnp.float32)
        else:
            low, high = power, jnp.zeros_like(power)
        own = jnp.concatenate([low, high], axis=1)
        far = jnp.concatenate([own[slabs // 2 :], own[: slabs // 2]], axis=0)
        for first in range(0, sent_ref.shape[0], 8 * slabs):
            sent_ref[pl.ds(first + part, slabs, stride=8), :] = own
            sent_ref[pl.ds(first + 4 + part, slabs, stride=8), :] = far


def prepare_kernel(
    slabs, slab_ref, x_group_ref, counts_ref, offsets_ref, strength_ref, cells_ref, kx_modes_ref, ky_modes_ref,
    sent_ref, x_ref, y_ref, fine_ref, mask_ref, power_ref, weight_ref, turn_ref,
):
    pack_rows(counts_ref, offsets_ref, strength_ref, cells_ref, sent_ref)

    slab, x_group = slab_ref[0], x_group_ref[0]
    kx_count, ky_count = x_ref.shape[1], y_ref.shape[1]

    def down_rows(modes, rows, first):
        lane = lax.broadcasted_iota(jnp.int32, (rows, modes.shape[1]), 1)
        row = lax.broadcasted_iota(jnp.int32, (rows, modes.shape[1]), 0)
        picked = jnp.sum(jnp.where(lane == row + first, modes, 0.0), axis=1, keepdims=True)
        return jnp.broadcast_to(picked, (rows, 128))

    ky_modes = ky_modes_ref[...].astype(jnp.float32)
    kx_rows = down_rows(kx_modes_ref[...].astype(jnp.float32), kx_count, x_group * kx_count)
    ky_rows = down_rows(ky_modes, ky_count, 0)
    ky_lanes = jnp.concatenate([ky_modes, ky_modes], axis=1)
    kx, ky = kx_rows * (1.0 / NXD), ky_rows * (1.0 / NXD)
    sigma = 4.0 / (ZDEV * slabs)
    step = 2.0 * math.pi / NXD
    signed_x = jnp.where(kx_rows >= NXD // 2, kx_rows - NXD, kx_rows)
    signed_y = jnp.where(ky_lanes >= NXD // 2, ky_lanes - NXD, ky_lanes)
    kappa = jnp.sqrt(sigma * sigma + step * step * (signed_x * signed_x + signed_y * signed_y))
    turns = (kx_rows + ky_lanes) * ((MIDDLE + 1.5) / NXD)

    row = lax.broadcasted_iota(jnp.int32, kx.shape, 0).astype(jnp.float32)
    key = jnp.abs(kx - jnp.round(kx)) * (NXD * kx_count) + row
    fine = []
    for j in range(FINE):
        chosen = key == jnp.min(key, axis=0, keepdims=True)
        key = jnp.where(chosen, 2.0 * NXD * kx_count, key)
        mask_ref[j] = jnp.where(chosen, 1.0, 0.0)
        fine.append(jnp.sum(jnp.where(chosen, kx, 0.0), axis=0, keepdims=True))
    fine_row = lax.broadcasted_iota(jnp.int32, (8, 128), 0)
    fine = jnp.where((fine_row & 1) == 0, fine[0], fine[1])

    columns = lax.broadcasted_iota(jnp.int32, (1, 128), 1).astype(jnp.float32)
    for freq, table_ref in ((kx, x_ref), (ky, y_ref), (fine, fine_ref)):
        for j, part in enumerate(cos_sin_turns(freq * columns) + node_phasors(freq)):
            table_ref[j] = part

    decay = jnp.exp(-kappa)
    power = jnp.ones_like(kappa)
    for z in range(ZDEV + 1):
        power_ref[z] = power
        power = power * decay

    half = slabs // 2
    first = jnp.where(slab >= half, half, 0)
    far_slab = jnp.where(slab >= half, slab - half, slab + half)
    for hop in range(half):
        target = first + partner(slab - first, hop, half)
        for j, source in enumerate((slab, far_slab)):
            ahead = target - source
            reach = jnp.where(
                ahead > 1, ZDEV * ahead - (PLANES - 1), jnp.where(ahead < 0, ZDEV * (-ahead - 1), 0)
            )
            weight = jnp.exp(-kappa * reach.astype(jnp.float32))
            for k, joins in enumerate((ahead == 1, ahead > 1, ahead < 0)):
                weight_ref[6 * hop + 3 * j + k] = jnp.where(joins, weight, 0.0)
    for j, source in enumerate((slab, far_slab)):
        weight_ref[6 * half + j] = jnp.full(kappa.shape, jnp.where(source < slabs - 1, 1.0, 0.0))

    scale = (sigma * 2.0 / NXD) / kappa
    turn_cos, turn_sin = cos_sin_turns(turns)
    real = lax.broadcasted_iota(jnp.int32, kappa.shape, 1) < kappa.shape[1] // 2
    turn_ref[0] = scale * turn_cos
    turn_ref[1] = scale * jnp.where(real, turn_sin, -turn_sin)


def spectrum_kernel(
    group, joined, rows_ref, x_ref, y_ref, fine_ref, mask_ref, power_ref, weight_ref, near_ref, *rest
):
    send_refs, (own_ref, far_ref) = rest[:-2], rest[-2:]
    kx_count = x_ref.shape[1]
    ky_count = y_ref.shape[1]
    blocks = rows_ref.shape[0] // 16
    low_lanes = lax.broadcasted_iota(jnp.int32, (8, 128), 1) < 64
    plane = lax.broadcasted_iota(jnp.int32, (40, 128), 0).astype(jnp.float32)
    fine_row = lax.broadcasted_iota(jnp.int32, (8, 128), 0)

    def operands(frac, cell, column, side, weights, row):
        strength = frac[row + 3 : row + 4]
        base_z = cell[row : row + 1]
        column_x, column_y = column[row + 1 : row + 2], column[row + 2 : row + 3]
        side_x, side_y = side[row + 1 : row + 2], side[row + 2 : row + 3]
        wz = [w[row : row + 1] * strength for w in weights]
        wx = node_pairs([w[row + 1 : row + 2] for w in weights])
        wy = node_pairs([w[row + 2 : row + 3].astype(jnp.bfloat16).astype(jnp.float32) for w in weights])
        dist = plane - base_z
        spread = jnp.where(
            dist == 0.0,
            wz[0],
            jnp.where(dist == 1.0, wz[1], jnp.where(dist == 2.0, wz[2], jnp.where(dist == 3.0, wz[3], 0.0))),
        )
        cx, sx = transform(x_ref, column_x, side_x, wx)
        cy, sy = transform(y_ref, column_y, side_y, wy)
        lhs = []
        for z in range(PLANES):
            here = jnp.broadcast_to(spread[z : z + 1], cx.shape)
            lhs.append(
                jnp.concatenate([(here * cx).astype(jnp.bfloat16), (here * sx).astype(jnp.bfloat16)], axis=1)
            )
        if row == 0:
            wz_rows = jnp.concatenate([w for w in wz for _ in range(FINE)], axis=0)
            deposited = [
                (wz_rows * w[row + 1 : row + 2]).astype(jnp.bfloat16).astype(jnp.float32) for w in weights
            ]
            fine_c, fine_s = lookup(fine_ref, column_x, side_x)
            exact = turned(fine_c, fine_s, fine_ref, node_pairs(deposited))
            plain = turned(fine_c, fine_s, fine_ref, wx)
            lacks = [
                e - (wz_rows * p).astype(jnp.bfloat16).astype(jnp.float32) for e, p in zip(exact, plain)
            ]
            shift = base_z.astype(jnp.int32) * FINE
            for z in range(0, spread.shape[0], 8):
                tiles = []
                for first in (z, z + 4):
                    if first >= PLANES:
                        tiles.append([jnp.zeros((8, 128), jnp.float32)] * 2)
                        continue
                    source = fine_row + FINE * first - shift
                    held = (source & 7) == source
                    tiles.append(
                        [jnp.where(held, jnp.take_along_axis(r, source & 7, axis=0), 0.0) for r in lacks]
                    )
                lhs.append(
                    jnp.concatenate(
                        [jnp.concatenate(pair, axis=0).astype(jnp.bfloat16) for pair in zip(*tiles)], axis=1
                    )
                )
        cy_high, cy_low = two_parts(cy)
        sy_high, sy_low = two_parts(-sy)
        rhs = [
            jnp.concatenate(pair, axis=1)
            for pair in ((cy_high, sy_high), (sy_high, -cy_high), (cy_low, sy_low), (sy_low, -cy_low))
        ]
        return jnp.concatenate(lhs, axis=0), jnp.concatenate(rhs, axis=0)

    def one_block(block):
        rows = rows_ref[pl.ds(pl.multiple_of(block * 16, 16), 16), :]
        rolled = pltpu.roll(rows, 64, axis=1)
        frac = jnp.where(low_lanes, rows[0:8], rolled[8:16])
        cell = jnp.where(low_lanes, rolled[0:8], rows[8:16])
        weights = node_weights(frac)
        column = jnp.abs(cell - MIDDLE).astype(jnp.int32)
        side = jnp.where(cell < MIDDLE, -1.0, 1.0)
        return tuple(operands(frac, cell, column, side, weights, row) for row in (0, 4))

    def step(index, _):
        pieces = [one_block(index * group + j) for j in range(group)]
        for part, acc_ref in enumerate((own_ref, far_ref)):
            lhs = jnp.concatenate([p[part][0] for p in pieces], axis=1)
            rhs = jnp.concatenate([p[part][1] for p in pieces], axis=1)
            product = lax.dot_general(
                lhs, rhs, (((1,), (1,)), ((), ())), preferred_element_type=jnp.float32
            )

            @pl.when(index == 0)
            def _():
                acc_ref[...] = product

            @pl.when(index > 0)
            def _():
                acc_ref[...] += product

        return 0

    lax.fori_loop(0, blocks // group, step, 0)

    decay = power_ref[1]
    width = 2 * ky_count

    def plane_of(acc_ref, z):
        both = acc_ref[z * kx_count : (z + 1) * kx_count, :]
        plane = both[:, :width] + both[:, width:]
        if acc_ref is own_ref:
            first = PLANES * kx_count + FINE * z
            for j in range(FINE):
                plane = plane + mask_ref[j] * acc_ref[first + j : first + j + 1, :width]
        return plane

    parts = []
    for j, acc_ref in enumerate((own_ref, far_ref)):
        inside = weight_ref[6 * len(send_refs) + j]
        spilled = [plane_of(acc_ref, ZDEV + k) * inside for k in range(SPILL)]
        down = spilled[0] + decay * (spilled[1] + decay * spilled[2])
        for z in range(ZDEV - 1, -1, -1):
            down = decay * down
            if j == 0:
                near_ref[z] = down
            down = plane_of(acc_ref, z) + down
        up = jnp.zeros_like(decay)
        for z in range(ZDEV):
            up = plane_of(acc_ref, z) + decay * up
            if j == 0:
                near_ref[z] += up
        up_near = spilled[0] + decay * up
        up_far = spilled[2] + decay * (spilled[1] + decay * up_near)
        parts.append((spilled, up_near, up_far, down))

    for hop, send_ref in enumerate(send_refs):
        low = high = first = second = 0.0
        for j, (spilled, up_near, up_far, down) in enumerate(parts):
            near_above, above, below = (weight_ref[6 * hop + 3 * j + k] for k in range(3))
            low = low + above * up_far
            high = high + below * down
            if joined[hop]:
                low = low + near_above * up_near
                first = first + near_above * spilled[1]
                second = second + near_above * spilled[2]
        send_ref[0] = low
        send_ref[1] = high
        if joined[hop]:
            send_ref[2] = first
            send_ref[3] = second


def far_kernel(power_ref, turn_ref, near_ref, *rest):
    received_refs, out_ref = rest[:-1], rest[-1]
    low, high, first, second = (
        sum(ref[part] for ref in received_refs if part < ref.shape[0]) for part in range(4)
    )
    decay = power_ref[1]
    turn_cos, turn_sin = turn_ref[0], turn_ref[1]
    low_at = [
        low + decay * (first + decay * second),
        decay * low + first + decay * second,
        decay * (decay * low + first) + second,
    ]
    for z in range(ZDEV):
        total = near_ref[z] + power_ref[ZDEV - z] * high
        total = total + (low_at[z] if z < 3 else power_ref[z - 2] * low_at[2])
        out_ref[z] = turn_cos * total + turn_sin * pltpu.roll(total, total.shape[1] // 2, axis=1)


def shards(offsets, strength, cells, counts, kx_modes, ky_modes):
    slabs = lax.axis_size("gz")
    x_groups = lax.axis_size("gx")
    half = slabs // 2
    cap = strength.shape[-1]
    kx_local = kx_modes.shape[0] // x_groups
    ky_count = ky_modes.shape[0]
    width = 2 * ky_count
    slab = lax.axis_index("gz").astype(jnp.int32).reshape(1)
    x_group = lax.axis_index("gx").astype(jnp.int32).reshape(1)

    smem = pl.BlockSpec(memory_space=pltpu.SMEM)
    vmem = pl.BlockSpec(memory_space=pltpu.VMEM)
    some = 16 * 1024 * 1024

    def shaped(*shape):
        return jax.ShapeDtypeStruct(shape, jnp.float32)

    prepared = (
        shaped(slabs * x_groups * 8, 2 * cap),
        shaped(6, kx_local, 128),
        shaped(6, ky_count, 128),
        shaped(6, 8, 128),
        shaped(FINE, kx_local, width),
        shaped(ZDEV + 1, kx_local, width),
        shaped(6 * half + 2, kx_local, width),
        shaped(2, kx_local, width),
    )
    inputs = (
        jnp.transpose(offsets[0], (1, 0, 2)),
        strength[0],
        jnp.transpose(cells[0], (1, 0, 2)),
        kx_modes.reshape(1, -1),
        ky_modes.reshape(1, -1),
    )
    sent, *tables, turn = pl.pallas_call(
        functools.partial(prepare_kernel, slabs),
        out_shape=prepared,
        in_specs=[smem] * 3 + [vmem] * len(inputs),
        out_specs=(vmem,) * len(prepared),
        compiler_params=pltpu.CompilerParams(vmem_limit_bytes=some),
    )(slab, x_group, *(pltpu.with_memory_space_constraint(array, pltpu.HBM) for array in (counts,) + inputs))
    powers = tables[4]
    sent = sent.reshape(slabs * x_groups, 8, 2 * cap)
    arrived = lax.all_to_all(sent, ("gx", "gz"), split_axis=0, concat_axis=0, tiled=True)
    arrived = arrived.reshape(-1, 128)

    blocks = arrived.shape[0] // 16
    group = math.gcd(blocks, 16)
    planes = shaped(ZDEV, kx_local, width)
    joined = [
        any(partner(m, hop, half) == (m + 1) % half for m in range(half)) for hop in range(half)
    ]
    coarse_rows = PLANES * kx_local
    fine_rows = FINE * 8 * pl.cdiv(PLANES, 8)
    near, *messages = pl.pallas_call(
        functools.partial(spectrum_kernel, group, joined),
        out_shape=(planes,) + tuple(shaped(4 if joins else 2, kx_local, width) for joins in joined),
        in_specs=[vmem] * (1 + len(tables)),
        out_specs=(vmem,) * (1 + half),
        scratch_shapes=[
            pltpu.VMEM((coarse_rows + fine_rows, 2 * width), jnp.float32),
            pltpu.VMEM((coarse_rows, 2 * width), jnp.float32),
        ],
        compiler_params=pltpu.CompilerParams(vmem_limit_bytes=40 * 1024 * 1024),
    )(arrived, *tables)

    received = messages[:1]
    for hop in range(1, half):
        pairs = [(i, i - i % half + partner(i % half, hop, half)) for i in range(slabs)]
        received.append(lax.ppermute(messages[hop], "gz", pairs))
    return pl.pallas_call(
        far_kernel,
        out_shape=planes,
        in_specs=[vmem] * (3 + half),
        out_specs=vmem,
        compiler_params=pltpu.CompilerParams(vmem_limit_bytes=some),
    )(powers, turn, near, *received)


def solution(mesh):
    placed = (
        P("gx", "gz", None, None),
        P("gx", "gz", None),
        P("gx", "gz", None, None),
        P("gx", "gz"),
        P(),
        P(),
    )
    return jax.shard_map(
        shards, mesh=mesh, in_specs=placed, out_specs=P("gz", "gx", None), check_vma=False
    )
```

```python
import functools
import math

import jax
import jax.numpy as jnp
from jax import lax
from jax.experimental import pallas as pl
from jax.experimental.pallas import tpu as pltpu
from jax.sharding import PartitionSpec as P

NXD = 512
ZDEV = 32
SPILL = 3
PLANES = ZDEV + SPILL
MIDDLE = 126.0
FINE = 2

SIN_HALF = tuple(math.sqrt(2.0) * c for c in (3.14158202, -5.16714279, 2.54189899, -0.55463611))
COS_HALF = tuple(math.sqrt(2.0) * c for c in (0.9999933, -4.93393801, 4.04128375, -1.22212681))


def poly(u, coefs):
    total = jnp.full_like(u, coefs[-1])
    for c in coefs[-2::-1]:
        total = total * u + c
    return total


def cos_sin_turns(turns):
    r = turns - jnp.round(turns)
    u = r * r
    s = r * poly(u, SIN_HALF)
    return 1.0 - s * s, s * poly(u, COS_HALF)


def node_weights(f):
    g = 1.0 - f
    fg = -0.5 * f * g
    return (
        fg * g,
        1.0 + f * f * (1.5 * f - 2.5),
        1.0 + g * g * (1.5 * g - 2.5),
        fg * f,
    )


def node_phasors(freq):
    return cos_sin_turns(0.5 * freq) + cos_sin_turns(1.5 * freq)


def lookup(table_ref, column, side):
    column = jnp.broadcast_to(column, table_ref.shape[1:])
    c = jnp.take_along_axis(table_ref[0], column, axis=1)
    return c, jnp.take_along_axis(table_ref[1], column, axis=1) * side


def turned(c, s, table_ref, pairs):
    even1, odd1, even3, odd3 = pairs
    re = even1 * table_ref[2] + even3 * table_ref[4]
    im = odd1 * table_ref[3] + odd3 * table_ref[5]
    return c * re - s * im, s * re + c * im


def transform(table_ref, column, side, pairs):
    return turned(*lookup(table_ref, column, side), table_ref, pairs)


def node_pairs(weights):
    w0, w1, w2, w3 = weights
    return w1 + w2, w2 - w1, w0 + w3, w3 - w0


def two_parts(x):
    high = x.astype(jnp.bfloat16)
    return high, (x - high.astype(jnp.float32)).astype(jnp.bfloat16)


def partner(index, step, count):
    return index ^ step if count & (count - 1) == 0 else (index + step) % count


def pack_rows(counts_ref, offsets_ref, strength_ref, cells_ref, sent_ref):
    slabs, cap = strength_ref.shape
    slot = lax.broadcasted_iota(jnp.int32, (slabs, cap), 0)
    lane = lax.broadcasted_iota(jnp.int32, (slabs, cap), 1)
    count = jnp.zeros((slabs, cap), jnp.int32)
    for d in range(slabs):
        count = jnp.where(slot == d, counts_ref[0, d], count)
    power = jnp.where(lane < count, strength_ref[...], 0.0)
    for part in range(4):
        if part < 3:
            low, high = offsets_ref[part], cells_ref[part].astype(jnp.float32)
        else:
            low, high = power, jnp.zeros_like(power)
        own = jnp.concatenate([low, high], axis=1)
        far = jnp.concatenate([own[slabs // 2 :], own[: slabs // 2]], axis=0)
        for first in range(0, sent_ref.shape[0], 8 * slabs):
            sent_ref[pl.ds(first + part, slabs, stride=8), :] = own
            sent_ref[pl.ds(first + 4 + part, slabs, stride=8), :] = far


def prepare_kernel(
    slabs, slab_ref, x_group_ref, counts_ref, offsets_ref, strength_ref, cells_ref, kx_modes_ref, ky_modes_ref,
    sent_ref, x_ref, y_ref, fine_ref, mask_ref, power_ref, weight_ref, turn_ref,
):
    pack_rows(counts_ref, offsets_ref, strength_ref, cells_ref, sent_ref)

    slab, x_group = slab_ref[0], x_group_ref[0]
    kx_count, ky_count = x_ref.shape[1], y_ref.shape[1]

    def down_rows(modes, rows, first):
        lane = lax.broadcasted_iota(jnp.int32, (rows, modes.shape[1]), 1)
        row = lax.broadcasted_iota(jnp.int32, (rows, modes.shape[1]), 0)
        picked = jnp.sum(jnp.where(lane == row + first, modes, 0.0), axis=1, keepdims=True)
        return jnp.broadcast_to(picked, (rows, 128))

    ky_modes = ky_modes_ref[...].astype(jnp.float32)
    kx_rows = down_rows(kx_modes_ref[...].astype(jnp.float32), kx_count, x_group * kx_count)
    ky_rows = down_rows(ky_modes, ky_count, 0)
    ky_lanes = jnp.concatenate([ky_modes, ky_modes], axis=1)
    kx, ky = kx_rows * (1.0 / NXD), ky_rows * (1.0 / NXD)
    sigma = 4.0 / (ZDEV * slabs)
    step = 2.0 * math.pi / NXD
    signed_x = jnp.where(kx_rows >= NXD // 2, kx_rows - NXD, kx_rows)
    signed_y = jnp.where(ky_lanes >= NXD // 2, ky_lanes - NXD, ky_lanes)
    kappa = jnp.sqrt(sigma * sigma + step * step * (signed_x * signed_x + signed_y * signed_y))
    turns = (kx_rows + ky_lanes) * ((MIDDLE + 1.5) / NXD)

    row = lax.broadcasted_iota(jnp.int32, kx.shape, 0).astype(jnp.float32)
    key = jnp.abs(kx - jnp.round(kx)) * (NXD * kx_count) + row
    fine = []
    for j in range(FINE):
        chosen = key == jnp.min(key, axis=0, keepdims=True)
        key = jnp.where(chosen, 2.0 * NXD * kx_count, key)
        mask_ref[j] = jnp.where(chosen, 1.0, 0.0)
        fine.append(jnp.sum(jnp.where(chosen, kx, 0.0), axis=0, keepdims=True))
    fine_row = lax.broadcasted_iota(jnp.int32, (8, 128), 0)
    fine = jnp.where((fine_row & 1) == 0, fine[0], fine[1])

    columns = lax.broadcasted_iota(jnp.int32, (1, 128), 1).astype(jnp.float32)
    for freq, table_ref in ((kx, x_ref), (ky, y_ref), (fine, fine_ref)):
        for j, part in enumerate(cos_sin_turns(freq * columns) + node_phasors(freq)):
            table_ref[j] = part

    decay = jnp.exp(-kappa)
    power = jnp.ones_like(kappa)
    for z in range(ZDEV + 1):
        power_ref[z] = power
        power = power * decay

    half = slabs // 2
    first = jnp.where(slab >= half, half, 0)
    far_slab = jnp.where(slab >= half, slab - half, slab + half)
    for hop in range(half):
        target = first + partner(slab - first, hop, half)
        for j, source in enumerate((slab, far_slab)):
            ahead = target - source
            reach = jnp.where(
                ahead > 1, ZDEV * ahead - (PLANES - 1), jnp.where(ahead < 0, ZDEV * (-ahead - 1), 0)
            )
            weight = jnp.exp(-kappa * reach.astype(jnp.float32))
            for k, joins in enumerate((ahead == 1, ahead > 1, ahead < 0)):
                weight_ref[6 * hop + 3 * j + k] = jnp.where(joins, weight, 0.0)
    for j, source in enumerate((slab, far_slab)):
        weight_ref[6 * half + j] = jnp.full(kappa.shape, jnp.where(source < slabs - 1, 1.0, 0.0))

    scale = (sigma * 2.0 / NXD) / kappa
    turn_cos, turn_sin = cos_sin_turns(turns)
    real = lax.broadcasted_iota(jnp.int32, kappa.shape, 1) < kappa.shape[1] // 2
    turn_ref[0] = scale * turn_cos
    turn_ref[1] = scale * jnp.where(real, turn_sin, -turn_sin)


def spectrum_kernel(
    group, joined, rows_ref, x_ref, y_ref, fine_ref, mask_ref, power_ref, weight_ref, near_ref, *rest
):
    send_refs, (own_ref, far_ref) = rest[:-2], rest[-2:]
    kx_count = x_ref.shape[1]
    ky_count = y_ref.shape[1]
    blocks = rows_ref.shape[0] // 16
    low_lanes = lax.broadcasted_iota(jnp.int32, (8, 128), 1) < 64
    plane = lax.broadcasted_iota(jnp.int32, (40, 128), 0).astype(jnp.float32)
    fine_row = lax.broadcasted_iota(jnp.int32, (8, 128), 0)

    def operands(frac, cell, column, side, weights, row):
        strength = frac[row + 3 : row + 4]
        base_z = cell[row : row + 1]
        column_x, column_y = column[row + 1 : row + 2], column[row + 2 : row + 3]
        side_x, side_y = side[row + 1 : row + 2], side[row + 2 : row + 3]
        wz = [w[row : row + 1] * strength for w in weights]
        wx = node_pairs([w[row + 1 : row + 2] for w in weights])
        wy = node_pairs([w[row + 2 : row + 3].astype(jnp.bfloat16).astype(jnp.float32) for w in weights])
        dist = plane - base_z
        spread = jnp.where(
            dist == 0.0,
            wz[0],
            jnp.where(dist == 1.0, wz[1], jnp.where(dist == 2.0, wz[2], jnp.where(dist == 3.0, wz[3], 0.0))),
        )
        cx, sx = transform(x_ref, column_x, side_x, wx)
        cy, sy = transform(y_ref, column_y, side_y, wy)
        lhs = []
        for z in range(PLANES):
            here = jnp.broadcast_to(spread[z : z + 1], cx.shape)
            lhs.append(
                jnp.concatenate([(here * cx).astype(jnp.bfloat16), (here * sx).astype(jnp.bfloat16)], axis=1)
            )
        if row == 0:
            wz_rows = jnp.concatenate([w for w in wz for _ in range(FINE)], axis=0)
            deposited = [
                (wz_rows * w[row + 1 : row + 2]).astype(jnp.bfloat16).astype(jnp.float32) for w in weights
            ]
            fine_c, fine_s = lookup(fine_ref, column_x, side_x)
            exact = turned(fine_c, fine_s, fine_ref, node_pairs(deposited))
            plain = turned(fine_c, fine_s, fine_ref, wx)
            lacks = [
                e - (wz_rows * p).astype(jnp.bfloat16).astype(jnp.float32) for e, p in zip(exact, plain)
            ]
            shift = base_z.astype(jnp.int32) * FINE
            for z in range(0, spread.shape[0], 8):
                tiles = []
                for first in (z, z + 4):
                    if first >= PLANES:
                        tiles.append([jnp.zeros((8, 128), jnp.float32)] * 2)
                        continue
                    source = fine_row + FINE * first - shift
                    held = (source & 7) == source
                    tiles.append(
                        [jnp.where(held, jnp.take_along_axis(r, source & 7, axis=0), 0.0) for r in lacks]
                    )
                lhs.append(
                    jnp.concatenate(
                        [jnp.concatenate(pair, axis=0).astype(jnp.bfloat16) for pair in zip(*tiles)], axis=1
                    )
                )
        cy_high, cy_low = two_parts(cy)
        sy_high, sy_low = two_parts(-sy)
        pairs = [(cy_high, sy_high), (sy_high, -cy_high)]
        if row == 0:
            pairs += [(cy_low, sy_low), (sy_low, -cy_low)]
        rhs = [jnp.concatenate(pair, axis=1) for pair in pairs]
        return jnp.concatenate(lhs, axis=0), jnp.concatenate(rhs, axis=0)

    def one_block(block):
        rows = rows_ref[pl.ds(pl.multiple_of(block * 16, 16), 16), :]
        rolled = pltpu.roll(rows, 64, axis=1)
        frac = jnp.where(low_lanes, rows[0:8], rolled[8:16])
        cell = jnp.where(low_lanes, rolled[0:8], rows[8:16])
        weights = node_weights(frac)
        column = jnp.abs(cell - MIDDLE).astype(jnp.int32)
        side = jnp.where(cell < MIDDLE, -1.0, 1.0)
        return tuple(operands(frac, cell, column, side, weights, row) for row in (0, 4))

    def step(index, _):
        pieces = [one_block(index * group + j) for j in range(group)]
        for part, acc_ref in enumerate((own_ref, far_ref)):
            lhs = jnp.concatenate([p[part][0] for p in pieces], axis=1)
            rhs = jnp.concatenate([p[part][1] for p in pieces], axis=1)
            product = lax.dot_general(
                lhs, rhs, (((1,), (1,)), ((), ())), preferred_element_type=jnp.float32
            )

            @pl.when(index == 0)
            def _():
                acc_ref[...] = product

            @pl.when(index > 0)
            def _():
                acc_ref[...] += product

        return 0

    lax.fori_loop(0, blocks // group, step, 0)

    decay = power_ref[1]
    width = 2 * ky_count

    def plane_of(acc_ref, z):
        both = acc_ref[z * kx_count : (z + 1) * kx_count, :]
        plane = both[:, :width] + both[:, width:] if acc_ref is own_ref else both
        if acc_ref is own_ref:
            first = PLANES * kx_count + FINE * z
            for j in range(FINE):
                plane = plane + mask_ref[j] * acc_ref[first + j : first + j + 1, :width]
        return plane

    parts = []
    for j, acc_ref in enumerate((own_ref, far_ref)):
        inside = weight_ref[6 * len(send_refs) + j]
        spilled = [plane_of(acc_ref, ZDEV + k) * inside for k in range(SPILL)]
        down = spilled[0] + decay * (spilled[1] + decay * spilled[2])
        for z in range(ZDEV - 1, -1, -1):
            down = decay * down
            if j == 0:
                near_ref[z] = down
            down = plane_of(acc_ref, z) + down
        up = jnp.zeros_like(decay)
        for z in range(ZDEV):
            up = plane_of(acc_ref, z) + decay * up
            if j == 0:
                near_ref[z] += up
        up_near = spilled[0] + decay * up
        up_far = spilled[2] + decay * (spilled[1] + decay * up_near)
        parts.append((spilled, up_near, up_far, down))

    for hop, send_ref in enumerate(send_refs):
        low = high = first = second = 0.0
        for j, (spilled, up_near, up_far, down) in enumerate(parts):
            near_above, above, below = (weight_ref[6 * hop + 3 * j + k] for k in range(3))
            low = low + above * up_far
            high = high + below * down
            if joined[hop]:
                low = low + near_above * up_near
                first = first + near_above * spilled[1]
                second = second + near_above * spilled[2]
        send_ref[0] = low
        send_ref[1] = high
        if joined[hop]:
            send_ref[2] = first
            send_ref[3] = second


def far_kernel(power_ref, turn_ref, near_ref, *rest):
    received_refs, out_ref = rest[:-1], rest[-1]
    low, high, first, second = (
        sum(ref[part] for ref in received_refs if part < ref.shape[0]) for part in range(4)
    )
    decay = power_ref[1]
    turn_cos, turn_sin = turn_ref[0], turn_ref[1]
    low_at = [
        low + decay * (first + decay * second),
        decay * low + first + decay * second,
        decay * (decay * low + first) + second,
    ]
    for z in range(ZDEV):
        total = near_ref[z] + power_ref[ZDEV - z] * high
        total = total + (low_at[z] if z < 3 else power_ref[z - 2] * low_at[2])
        out_ref[z] = turn_cos * total + turn_sin * pltpu.roll(total, total.shape[1] // 2, axis=1)


def shards(offsets, strength, cells, counts, kx_modes, ky_modes):
    slabs = lax.axis_size("gz")
    x_groups = lax.axis_size("gx")
    half = slabs // 2
    cap = strength.shape[-1]
    kx_local = kx_modes.shape[0] // x_groups
    ky_count = ky_modes.shape[0]
    width = 2 * ky_count
    slab = lax.axis_index("gz").astype(jnp.int32).reshape(1)
    x_group = lax.axis_index("gx").astype(jnp.int32).reshape(1)

    smem = pl.BlockSpec(memory_space=pltpu.SMEM)
    vmem = pl.BlockSpec(memory_space=pltpu.VMEM)
    some = 16 * 1024 * 1024

    def shaped(*shape):
        return jax.ShapeDtypeStruct(shape, jnp.float32)

    prepared = (
        shaped(slabs * x_groups * 8, 2 * cap),
        shaped(6, kx_local, 128),
        shaped(6, ky_count, 128),
        shaped(6, 8, 128),
        shaped(FINE, kx_local, width),
        shaped(ZDEV + 1, kx_local, width),
        shaped(6 * half + 2, kx_local, width),
        shaped(2, kx_local, width),
    )
    inputs = (
        jnp.transpose(offsets[0], (1, 0, 2)),
        strength[0],
        jnp.transpose(cells[0], (1, 0, 2)),
        kx_modes.reshape(1, -1),
        ky_modes.reshape(1, -1),
    )
    sent, *tables, turn = pl.pallas_call(
        functools.partial(prepare_kernel, slabs),
        out_shape=prepared,
        in_specs=[smem] * 3 + [vmem] * len(inputs),
        out_specs=(vmem,) * len(prepared),
        compiler_params=pltpu.CompilerParams(vmem_limit_bytes=some),
    )(slab, x_group, *(pltpu.with_memory_space_constraint(array, pltpu.HBM) for array in (counts,) + inputs))
    powers = tables[4]
    sent = sent.reshape(slabs * x_groups, 8, 2 * cap)
    arrived = lax.all_to_all(sent, ("gx", "gz"), split_axis=0, concat_axis=0, tiled=True)
    arrived = arrived.reshape(-1, 128)

    blocks = arrived.shape[0] // 16
    group = math.gcd(blocks, 16)
    planes = shaped(ZDEV, kx_local, width)
    joined = [
        any(partner(m, hop, half) == (m + 1) % half for m in range(half)) for hop in range(half)
    ]
    coarse_rows = PLANES * kx_local
    fine_rows = FINE * 8 * pl.cdiv(PLANES, 8)
    near, *messages = pl.pallas_call(
        functools.partial(spectrum_kernel, group, joined),
        out_shape=(planes,) + tuple(shaped(4 if joins else 2, kx_local, width) for joins in joined),
        in_specs=[vmem] * (1 + len(tables)),
        out_specs=(vmem,) * (1 + half),
        scratch_shapes=[
            pltpu.VMEM((coarse_rows + fine_rows, 2 * width), jnp.float32),
            pltpu.VMEM((coarse_rows, width), jnp.float32),
        ],
        compiler_params=pltpu.CompilerParams(vmem_limit_bytes=40 * 1024 * 1024),
    )(arrived, *tables)

    received = messages[:1]
    for hop in range(1, half):
        pairs = [(i, i - i % half + partner(i % half, hop, half)) for i in range(slabs)]
        received.append(lax.ppermute(messages[hop], "gz", pairs))
    return pl.pallas_call(
        far_kernel,
        out_shape=planes,
        in_specs=[vmem] * (3 + half),
        out_specs=vmem,
        compiler_params=pltpu.CompilerParams(vmem_limit_bytes=some),
    )(powers, turn, near, *received)


def solution(mesh):
    placed = (
        P("gx", "gz", None, None),
        P("gx", "gz", None),
        P("gx", "gz", None, None),
        P("gx", "gz"),
        P(),
        P(),
    )
    return jax.shard_map(
        shards, mesh=mesh, in_specs=placed, out_specs=P("gz", "gx", None), check_vma=False
    )
```
